128 devices in a mesh: blk: 32 (over z_lo, x, y), dp: 4 (over z_hi, core).
Axes of the slice: x: 4, y: 4, z: 4 (z_hi: 2, z_lo: 2; z = z_hi * 2 + z_lo), core: 2. Of those that a mesh axis runs over, the one named last changes fastest.
Arguments:
- segment_sums: bfloat16 [16384, 4096], P(('blk', 'dp')), may hold values from -240 to 240, as said below
- lengths: int32 [16384], P(('blk', 'dp')), may hold values from 8 to 128
- targets: int32 [16384], P(('blk', 'dp')), may hold values from 0 to 16383, as said below
- tile_masks: int32 [128, 2, 2, 2], P(('blk', 'dp')), may hold values from 0 to 1
Outputs:
- pair_losses: float32 [8192], P(('blk', 'dp'))
- sum_gradients: bfloat16 [16384, 4096], P(('blk', 'dp'))
The draws below stay inside these ranges and needn't reach their ends.
Inputs may be any that keep to these rules, and one draw needn't show every extreme that they name: segment_sums is finite. `targets`: a permutation of the 16384 slots; segment n belongs to owner n // 128 and slot g to loss shard g // 128, both in the order blk then dp; at most 2 segments of one owner go to one loss shard, and every loss shard receives exactly 2 from one owner.
All inputs are finite; a program needn't handle non-finite values.
Results may differ from the reference program's by a relative error of at most 0.0051.
Values may be sent and summed in bfloat16 or wider, within the bound.
A program may use at most 64 MiB of HBM per device.

```python
import math
import jax
import jax.numpy as jnp
from jax import lax

D = 4096
SEG_DEV = 128
STOPS = 2
TILES = 2
PAIRS = 64
TILE = 32
CAP = 2
SEGMENTS = 16384
TOTAL_PAIRS = 8192
N_BLK = 32
N_DP = 4
DEVICES = 128


def shared_lengths(key):
    key = jax.random.fold_in(key, 11)
    return jax.random.randint(key, (SEGMENTS,), 8, 129, dtype=jnp.int32)


def shared_targets(key):
    key = jax.random.fold_in(key, 23)
    offset_key, spread_key, source_key, receiver_key = jax.random.split(key, 4)
    average = SEG_DEV // DEVICES
    spare_room = CAP - average
    offsets = jax.random.permutation(offset_key, DEVICES).astype(jnp.int32)
    wiggle = jax.random.randint(spread_key, (DEVICES // 2,), -spare_room, spare_room + 1, dtype=jnp.int32)
    wiggle = wiggle.at[0].set(spare_room)
    counts = jnp.stack([average + wiggle, average - wiggle], 1).reshape(DEVICES)
    bounds = jnp.cumsum(counts)
    places = jnp.arange(SEG_DEV, dtype=jnp.int32)
    section_index = jnp.sum((bounds[None, :] <= places[:, None]).astype(jnp.int32), axis=1)
    sources = jnp.arange(DEVICES, dtype=jnp.int32)
    receivers = (sources[:, None] + offsets[section_index][None, :]) % DEVICES
    source_order = jax.vmap(lambda single: jax.random.permutation(single, SEG_DEV))(jax.random.split(source_key, DEVICES)).astype(jnp.int32)
    receiver_order = jax.vmap(lambda single: jax.random.permutation(single, SEG_DEV))(jax.random.split(receiver_key, DEVICES)).astype(jnp.int32)
    segment_index = sources[:, None] * SEG_DEV + source_order
    slot_index = receivers * SEG_DEV + receiver_order[receivers, jnp.broadcast_to(places[None, :], receivers.shape)]
    return jnp.zeros((SEGMENTS,), jnp.int32).at[segment_index.reshape(-1)].set(slot_index.reshape(-1))


def draw_lengths(key, part):
    return shared_lengths(key)


def draw_targets(key, part):
    return shared_targets(key)


def draw_tile_masks(key, part):
    key = jax.random.fold_in(key, 37)
    level_key, cell_key = jax.random.split(key)
    levels = jax.random.randint(level_key, (DEVICES, 1, 1, 1), 1, 5, dtype=jnp.int32)
    cell_draws = jax.random.randint(cell_key, (DEVICES, STOPS, TILES, TILES), 0, 4, dtype=jnp.int32)
    return (cell_draws < levels).astype(jnp.int32)


def draw_segment_sums(key, part):
    length_draw = shared_lengths(key)
    key = jax.random.fold_in(key, 5)
    base_key = jax.random.fold_in(key, 0)
    length_values = length_draw.astype(jnp.float32)
    root_lengths = jnp.sqrt(length_values)[:, None]
    drawn_sums = root_lengths * jax.random.truncated_normal(base_key, -6.0, 6.0, (SEGMENTS, D), jnp.float32)
    return drawn_sums.astype(jnp.bfloat16)


def setup_inputs(seed: int = 0) -> dict:
    arg_keys = jax.random.split(jax.random.key(seed), 5)
    return {
        "segment_sums": draw_segment_sums(jax.random.fold_in(arg_keys[4], 71), 0),
        "lengths": draw_lengths(jax.random.fold_in(arg_keys[4], 71), 0),
        "targets": draw_targets(jax.random.fold_in(arg_keys[4], 71), 0),
        "tile_masks": draw_tile_masks(jax.random.fold_in(arg_keys[4], 71), 0),
    }


def live_mask(tile_bits):
    diagonal = jnp.eye(TILES, dtype=jnp.int32)
    first_stop = jnp.maximum(tile_bits[0], diagonal)
    both_stops = jnp.concatenate([first_stop, tile_bits[1]], axis=1)
    return jnp.repeat(jnp.repeat(both_stops, TILE, 0), TILE, 1) > 0

def reference(segment_sums, lengths, targets, tile_masks):
    factor = 16.0 / math.sqrt(D)
    coefficient = factor / TOTAL_PAIRS
    embedded = (segment_sums.astype(jnp.float32) / lengths.astype(jnp.float32)[:, None]).astype(jnp.bfloat16)
    inverse = jnp.zeros((SEGMENTS,), jnp.int32).at[targets].set(jnp.arange(SEGMENTS, dtype=jnp.int32))
    placed = embedded[inverse].reshape(DEVICES, PAIRS, 2, D)
    queries = placed[:, :, 0]
    documents = placed[:, :, 1]
    slot_lengths = lengths[inverse].astype(jnp.float32).reshape(DEVICES, PAIRS, 2)
    shard_ids = jnp.arange(DEVICES, dtype=jnp.int32)
    neighbour = (shard_ids // N_DP - 1) % N_BLK * N_DP + shard_ids % N_DP
    successor = (shard_ids // N_DP + 1) % N_BLK * N_DP + shard_ids % N_DP

    def shard_scores(shard):
        candidates = jnp.concatenate([documents[shard], documents[neighbour[shard]]], 0)
        scores = factor * jnp.dot(queries[shard], candidates.T, preferred_element_type=jnp.float32)
        return (jnp.where(live_mask(tile_masks[shard]), scores, -jnp.inf), candidates)

    def row_stats(shard):
        scores, candidates = shard_scores(shard)
        highest = lax.optimization_barrier(jnp.max(scores, axis=1, keepdims=True))
        log_total = highest[:, 0] + jnp.log(lax.optimization_barrier(jnp.sum(jnp.exp(scores - highest), axis=1)))
        return (log_total, log_total - jnp.diagonal(scores[:, :PAIRS]))
    log_totals, losses = lax.map(row_stats, shard_ids)

    def gradients(shard):
        scores, candidates = shard_scores(shard)
        weights = jnp.where(jnp.isfinite(scores), jnp.exp(scores - log_totals[shard][:, None]), 0.0).astype(jnp.bfloat16)
        own_docs = documents[shard]
        own_queries = queries[shard]
        query_grads = coefficient * (jnp.dot(weights, candidates, preferred_element_type=jnp.float32) - own_docs.astype(jnp.float32))
        own_term = jnp.dot(weights[:, :PAIRS].T, own_queries, preferred_element_type=jnp.float32)
        later = successor[shard]
        later_queries = queries[later]
        later_scores = factor * jnp.dot(later_queries, own_docs.T, preferred_element_type=jnp.float32)
        later_live = live_mask(tile_masks[later])[:, PAIRS:]
        later_weights = jnp.where(later_live, jnp.exp(later_scores - log_totals[later][:, None]), 0.0).astype(jnp.bfloat16)
        far_term = jnp.dot(later_weights.T, later_queries, preferred_element_type=jnp.float32)
        doc_grads = coefficient * (own_term - own_queries.astype(jnp.float32)) + coefficient * far_term
        slot_grads = jnp.stack([query_grads, doc_grads], 1) / slot_lengths[shard][:, :, None]
        return slot_grads.astype(jnp.bfloat16).reshape(SEG_DEV, D)
    slot_all = lax.map(gradients, shard_ids).reshape(SEGMENTS, D)
    return (losses.reshape(TOTAL_PAIRS), slot_all[targets])
```

```python
import functools
import math

import jax
import jax.numpy as jnp
from jax import lax
from jax.experimental import pallas as pl
from jax.experimental.pallas import tpu as pltpu
from jax.sharding import PartitionSpec as P

MESH = pl.DeviceIdType.MESH
GROUP = 8
WIDE = 512
RINGS = 16
DEVICES = 128
ROWS = 128
PAIRS = 64
MSG = 16
F32 = jnp.float32
BF16 = jnp.bfloat16


def iota(shape, dim):
    return lax.broadcasted_iota(jnp.int32, shape, dim)


def nt_dot(a, b):
    return lax.dot_general(a, b, (((1,), (1,)), ((), ())), preferred_element_type=F32)


def tn_dot(a, b):
    return lax.dot_general(a, b, (((0,), (0,)), ((), ())), preferred_element_type=F32)


def nn_dot(a, b):
    return jnp.dot(a, b, preferred_element_type=F32)


def one_hot(mask):
    return jnp.where(mask, 1.0, 0.0).astype(BF16)


def place(part, ring):
    return (ring // 4) * 8 + part, ring % 4


def kernel(
    factor,
    coefficient,
    sums_ref,
    lengths_ref,
    targets_ref,
    masks_ref,
    loss_ref,
    out_ref,
    send_one_hot,
    back_one_hot,
    sent,
    landed,
    meta_out,
    meta,
    codes,
    place_one_hot,
    return_one_hot,
    inverse,
    queries,
    documents,
    partial,
    gathered,
    weights,
    totals,
    gradients,
    returning,
    returned,
    send_sem,
    land_sem,
    meta_send_sem,
    meta_sem,
    spread_send_sem,
    spread_sem,
    side_send_sem,
    side_sem,
    score_send_sem,
    score_sem,
    weight_send_sem,
    weight_sem,
    back_send_sem,
    back_sem,
):
    blk = lax.axis_index("blk")
    dp = lax.axis_index("dp")
    part = blk % 8
    ring = (blk // 8) * 4 + dp
    me = part * 16 + ring

    def remote(src, dst, send, recv, to_part, to_ring):
        return pltpu.make_async_remote_copy(
            src_ref=src,
            dst_ref=dst,
            send_sem=send,
            recv_sem=recv,
            device_id=place(to_part, to_ring),
            device_id_type=MESH,
        )

    barrier = pltpu.get_barrier_semaphore()

    def greet(step, carry):
        other = (me + step) % DEVICES
        pl.semaphore_signal(
            barrier, inc=1, device_id=place(other // 16, other % 16), device_id_type=MESH
        )
        return carry

    lax.fori_loop(1, DEVICES, greet, 0)

    target = targets_ref[...]
    length = lengths_ref[...].astype(F32)
    shard = target // ROWS
    slot = target % ROWS
    block = shard // 4
    to_ring = (block // 8) * 4 + shard % 4
    of_shard = one_hot(iota((DEVICES, ROWS), 0) == shard)
    earlier = one_hot(iota((ROWS, ROWS), 0) < iota((ROWS, ROWS), 1))
    before = nn_dot(of_shard, earlier)
    rank = jnp.sum(before * of_shard.astype(F32), axis=0, keepdims=True).astype(jnp.int32)
    inner = (block % 8) * 2 + rank
    position = to_ring * MSG + inner
    send_one_hot[...] = one_hot(iota((2 * ROWS, ROWS), 0) == position)
    column = jnp.transpose(jnp.broadcast_to(position.astype(F32), (ROWS, ROWS))).astype(jnp.int32)
    lanes = iota((ROWS, ROWS), 1)
    back_one_hot[:, :ROWS] = one_hot(column == lanes)
    back_one_hot[:, ROWS:] = one_hot(column == lanes + ROWS)
    code = ((slot % 2) * PAIRS + slot // 2 + 1).astype(F32)
    mine = iota((RINGS, ROWS), 0) == to_ring
    spot = one_hot(iota((ROWS, ROWS), 0) == (ring % 8) * MSG + inner)
    code_rows = nt_dot(jnp.where(mine, code, 0.0).astype(BF16), spot)
    length_rows = nt_dot(jnp.where(mine, length, 0.0).astype(BF16), spot)
    for g in range(RINGS):
        meta_out[g, 0:1, :] = code_rows[g : g + 1]
        meta_out[g, 1:2, :] = length_rows[g : g + 1]
    scale = 1.0 / jnp.transpose(jnp.broadcast_to(length, (ROWS, ROWS)))
    scale = jnp.concatenate([scale] * (WIDE // ROWS), axis=1)

    def pack(step, carry):
        k = (part + step) % GROUP
        columns = sums_ref[:, pl.ds(pl.multiple_of(k * WIDE, WIDE), WIDE)].astype(F32)
        embedded = (columns * scale).astype(BF16)
        sent[k] = nn_dot(send_one_hot[...], embedded).astype(BF16)
        return carry

    lax.fori_loop(0, GROUP, pack, 0)

    pl.semaphore_wait(barrier, DEVICES - 1)

    def meta_hop(step, carry):
        g = (ring + step) % RINGS
        src, dst = meta_out.at[g], meta.at[ring % 8, part * 2 + ring // 8]

        @pl.when((g == ring) & (part == ring % 8))
        def _():
            pltpu.make_async_copy(src, dst, meta_sem).start()

        @pl.when(jnp.logical_not((g == ring) & (part == ring % 8)))
        def _():
            remote(src, dst, meta_send_sem, meta_sem, ring % 8, g).start()

        return carry

    lax.fori_loop(0, RINGS, meta_hop, 0)

    def rows_out(step, carry):
        k = (part + step // RINGS) % GROUP
        g = (ring + step % RINGS) % RINGS
        src = sent.at[k, pl.ds(pl.multiple_of(g * MSG, MSG), MSG)]
        dst = landed.at[pl.ds(pl.multiple_of(me * MSG, MSG), MSG)]
        remote(src, dst, send_sem, land_sem.at[part], k, g).start()
        return carry

    pltpu.make_async_copy(
        sent.at[part, pl.ds(pl.multiple_of(ring * MSG, MSG), MSG)],
        landed.at[pl.ds(pl.multiple_of(me * MSG, MSG), MSG)],
        land_sem.at[part],
    ).start()
    lax.fori_loop(1, DEVICES, rows_out, 0)

    pltpu.make_async_copy(meta.at[part], meta.at[part], meta_sem).wait()

    def spread(step, carry):
        k = (part + step) % GROUP
        remote(
            meta.at[part], meta.at[part], spread_send_sem.at[step], spread_sem.at[part], k, ring
        ).start()
        return carry

    lax.fori_loop(1, GROUP, spread, 0)

    def spread_wait(step, carry):
        k = (part + GROUP - step) % GROUP
        remote(
            meta.at[k], meta.at[k], spread_send_sem.at[step], spread_sem.at[k], k, ring
        ).wait_recv()
        return carry

    lax.fori_loop(1, GROUP, spread_wait, 0)
    both = meta[0]
    for k in range(1, GROUP):
        both = both + meta[k]
    codes[...] = both

    inner_shard = (iota((1, ROWS), 1) % MSG) // 2

    def build(a, total):
        pair = codes[a]
        raw = pair[0:1].astype(jnp.int32) - 1
        live = jnp.where(raw >= PAIRS, 7 * PAIRS + raw, raw) + inner_shard * PAIRS
        full = jnp.where(raw >= 0, live, -1)
        matrix = one_hot(iota((8 * ROWS, ROWS), 0) == full)
        place_one_hot[a] = matrix
        down = jnp.transpose(jnp.broadcast_to(full.astype(F32), (ROWS, ROWS))).astype(jnp.int32)
        for s in range(GROUP):
            return_one_hot[pl.ds(pl.multiple_of(a * ROWS, ROWS), ROWS), s * ROWS : (s + 1) * ROWS] = (
                one_hot(down == lanes + s * ROWS)
            )
        wide = jnp.broadcast_to(pair[1:2], (ROWS, ROWS)).astype(BF16)
        inverse[...] = jnp.where(a == 0, 0.0, inverse[...]) + nt_dot(matrix, wide)
        return total

    inverse[...] = jnp.zeros(inverse.shape, F32)
    lax.fori_loop(0, 16, build, 0)
    inverse[...] = coefficient / inverse[...]

    def rows_wait(step, carry):
        k = (part + GROUP - step) % GROUP
        chunk = landed.at[pl.ds(pl.multiple_of(k * 256, 256), 256)]
        pltpu.make_async_copy(chunk, chunk, land_sem.at[k]).wait()
        return carry

    lax.fori_loop(0, GROUP, rows_wait, 0)

    def put(half):
        matrix = jnp.concatenate(
            [place_one_hot[a, half * 512 : (half + 1) * 512] for a in range(16)], axis=1
        )
        return nn_dot(matrix, landed[...]).astype(BF16)

    documents[PAIRS:] = put(1)
    queries[: 8 * PAIRS] = put(0)

    after = (ring + 4) % RINGS
    ahead = (ring + 12) % RINGS
    to_next = remote(
        documents.at[8 * PAIRS :], documents.at[:PAIRS], side_send_sem.at[0], side_sem.at[0], part, after
    )
    to_last = remote(
        queries.at[:PAIRS], queries.at[8 * PAIRS :], side_send_sem.at[1], side_sem.at[1], part, ahead
    )
    to_next.start()
    to_last.start()

    to_next.wait_recv()

    def score(step, carry):
        s = (part + step) % GROUP
        rows = queries[pl.ds(pl.multiple_of(s * PAIRS, PAIRS), PAIRS)]
        others = documents[pl.ds(pl.multiple_of(s * PAIRS, PAIRS), 2 * PAIRS)]
        partial[s] = nt_dot(rows, others)
        remote(
            partial.at[s], gathered.at[part], score_send_sem.at[step], score_sem.at[part], s, ring
        ).start()
        return carry

    lax.fori_loop(1, GROUP, score, 0)
    own_rows = queries[pl.ds(pl.multiple_of(part * PAIRS, PAIRS), PAIRS)]
    own_others = documents[pl.ds(pl.multiple_of(part * PAIRS, PAIRS), 2 * PAIRS)]
    gathered[part] = nt_dot(own_rows, own_others)

    def score_wait(step, carry):
        k = (part + GROUP - step) % GROUP
        remote(
            partial.at[k], gathered.at[k], score_send_sem.at[step], score_sem.at[k], k, ring
        ).wait_recv()
        return carry

    lax.fori_loop(1, GROUP, score_wait, 0)
    scores = gathered[0]
    for k in range(1, GROUP):
        scores = scores + gathered[k]
    scores = factor * scores

    row = iota((PAIRS, 2 * PAIRS), 0)
    col = iota((PAIRS, 2 * PAIRS), 1)

    def tile(stop, i, j):
        return masks_ref[stop * 4 + i * 2 + j]

    top = jnp.where(
        col < 32,
        tile(1, 0, 0),
        jnp.where(col < 64, tile(1, 0, 1), jnp.where(col < 96, 1, tile(0, 0, 1))),
    )
    low = jnp.where(
        col < 32,
        tile(1, 1, 0),
        jnp.where(col < 64, tile(1, 1, 1), jnp.where(col < 96, tile(0, 1, 0), 1)),
    )
    live = jnp.where(row < 32, top, low) > 0
    masked = jnp.where(live, scores, -jnp.inf)
    highest = jnp.max(masked, axis=1, keepdims=True)
    log_total = highest + jnp.log(jnp.sum(jnp.exp(masked - highest), axis=1, keepdims=True))
    diagonal = jnp.sum(jnp.where(col == row + PAIRS, scores, 0.0), axis=1, keepdims=True)
    losses = jnp.where(col == row, log_total - diagonal, 0.0)
    loss_ref[...] = jnp.sum(losses, axis=0, keepdims=True)[:, :PAIRS]
    weights[part] = jnp.exp(masked - log_total).astype(BF16)

    def weight_out(step, carry):
        s = (part + step) % GROUP
        remote(
            weights.at[part], weights.at[part], weight_send_sem.at[step], weight_sem.at[part], s, ring
        ).start()
        return carry

    lax.fori_loop(1, GROUP, weight_out, 0)

    @pl.when(part == 0)
    def _():
        def far_out(step, carry):
            remote(
                weights.at[0], weights.at[8], weight_send_sem.at[8 + step], weight_sem.at[8], step, ahead
            ).start()
            return carry

        lax.fori_loop(0, GROUP, far_out, 0)

    def weight_wait(step, carry):
        k = (part + GROUP - step) % GROUP
        remote(
            weights.at[k], weights.at[k], weight_send_sem.at[step], weight_sem.at[k], k, ring
        ).wait_recv()
        return carry

    lax.fori_loop(1, GROUP, weight_wait, 0)
    remote(weights.at[0], weights.at[8], weight_send_sem.at[8], weight_sem.at[8], 0, ahead).wait_recv()
    to_last.wait_recv()

    def spread_scale(value):
        return jnp.concatenate([value] * (WIDE // ROWS), axis=1)

    def gradient(s, carry):
        start = pl.multiple_of(s * PAIRS, PAIRS)
        one = pl.ds(start, PAIRS)
        after_one = pl.ds(pl.multiple_of(s * PAIRS + PAIRS, PAIRS), PAIRS)
        two = pl.ds(start, 2 * PAIRS)
        weight = weights[s]
        term = nn_dot(weight, documents[two]) - documents[after_one].astype(F32)
        gradients[one] = (term * spread_scale(inverse[one])).astype(BF16)
        far = tn_dot(weight, queries[one])
        totals[one] = totals[one] + far[:PAIRS]
        totals[after_one] = far[PAIRS:] - queries[one].astype(F32)
        return carry

    totals[:PAIRS] = jnp.zeros((PAIRS, WIDE), F32)
    lax.fori_loop(0, GROUP, gradient, 0)
    totals[8 * PAIRS :] = totals[8 * PAIRS :] + tn_dot(weights[8], queries[8 * PAIRS :])[:PAIRS]
    gradients[8 * PAIRS :] = (totals[PAIRS:] * spread_scale(inverse[8 * PAIRS :])).astype(BF16)

    def rows_back(step, carry):
        k = (part + step) % GROUP
        rows = pl.ds(pl.multiple_of(k * 256, 256), 256)
        returning[rows] = nn_dot(return_one_hot[rows], gradients[...]).astype(BF16)

        def one(turn, inner_carry):
            g = (ring + turn) % RINGS
            src = returning.at[pl.ds(pl.multiple_of((k * 16 + g) * MSG, MSG), MSG)]
            dst = returned.at[part, pl.ds(pl.multiple_of(ring * MSG, MSG), MSG)]
            remote(src, dst, back_send_sem, back_sem.at[part], k, g).start()
            return inner_carry

        @pl.when(step == 0)
        def _():
            pltpu.make_async_copy(
                returning.at[pl.ds(pl.multiple_of(me * MSG, MSG), MSG)],
                returned.at[part, pl.ds(pl.multiple_of(ring * MSG, MSG), MSG)],
                back_sem.at[part],
            ).start()

        lax.fori_loop(jnp.where(step == 0, 1, 0), RINGS, one, 0)
        return carry

    lax.fori_loop(0, GROUP, rows_back, 0)

    def finish(step, carry):
        k = (part + GROUP - step) % GROUP
        pltpu.make_async_copy(returned.at[k], returned.at[k], back_sem.at[k]).wait()
        out_ref[:, pl.ds(pl.multiple_of(k * WIDE, WIDE), WIDE)] = nn_dot(
            back_one_hot[...], returned[k]
        ).astype(BF16)
        return carry

    lax.fori_loop(0, GROUP, finish, 0)

    most = landed.at[pl.ds(0, (DEVICES - 1) * MSG)]
    pltpu.make_async_copy(most, most, send_sem).wait()
    pltpu.make_async_copy(most, most, back_send_sem).wait()

    @pl.when(part == ring % 8)
    def _():
        fifteen = meta_out.at[pl.ds(0, RINGS - 1)]
        pltpu.make_async_copy(fifteen, fifteen, meta_send_sem).wait()

    @pl.when(part != ring % 8)
    def _():
        pltpu.make_async_copy(meta_out, meta_out, meta_send_sem).wait()

    to_next.wait_send()
    to_last.wait_send()

    def sent_wait(step, carry):
        k = (part + step) % GROUP
        remote(
            meta.at[part], meta.at[part], spread_send_sem.at[step], spread_sem.at[part], k, ring
        ).wait_send()
        remote(
            partial.at[k], gathered.at[part], score_send_sem.at[step], score_sem.at[part], k, ring
        ).wait_send()
        remote(
            weights.at[part], weights.at[part], weight_send_sem.at[step], weight_sem.at[part], k, ring
        ).wait_send()
        return carry

    lax.fori_loop(1, GROUP, sent_wait, 0)

    @pl.when(part == 0)
    def _():
        def far_wait(step, carry):
            remote(
                weights.at[0], weights.at[8], weight_send_sem.at[8 + step], weight_sem.at[8], step, ahead
            ).wait_send()
            return carry

        lax.fori_loop(0, GROUP, far_wait, 0)


def local(segment_sums, lengths, targets, tile_masks):
    width = segment_sums.shape[1]
    factor = 16.0 / math.sqrt(width)
    coefficient = factor / (PAIRS * DEVICES)
    vmem = pl.BlockSpec(memory_space=pltpu.VMEM)
    smem = pl.BlockSpec(memory_space=pltpu.SMEM)
    dma = pltpu.SemaphoreType.DMA
    losses, gradients = pl.pallas_call(
        functools.partial(kernel, factor, coefficient),
        out_shape=(
            jax.ShapeDtypeStruct((1, PAIRS), F32),
            jax.ShapeDtypeStruct((ROWS, width), BF16),
        ),
        in_specs=[vmem, vmem, vmem, smem],
        out_specs=(vmem, vmem),
        scratch_shapes=[
            pltpu.VMEM((2 * ROWS, ROWS), BF16),
            pltpu.VMEM((ROWS, 2 * ROWS), BF16),
            pltpu.VMEM((GROUP, 2 * ROWS, WIDE), BF16),
            pltpu.VMEM((DEVICES * MSG, WIDE), BF16),
            pltpu.VMEM((RINGS, 2, ROWS), F32),
            pltpu.VMEM((GROUP, 16, 2, ROWS), F32),
            pltpu.VMEM((16, 2, ROWS), F32),
            pltpu.VMEM((16, GROUP * ROWS, ROWS), BF16),
            pltpu.VMEM((DEVICES * MSG, GROUP * ROWS), BF16),
            pltpu.VMEM((GROUP * ROWS, ROWS), F32),
            pltpu.VMEM((9 * PAIRS, WIDE), BF16),
            pltpu.VMEM((9 * PAIRS, WIDE), BF16),
            pltpu.VMEM((GROUP, PAIRS, 2 * PAIRS), F32),
            pltpu.VMEM((GROUP, PAIRS, 2 * PAIRS), F32),
            pltpu.VMEM((9, PAIRS, 2 * PAIRS), BF16),
            pltpu.VMEM((9 * PAIRS, WIDE), F32),
            pltpu.VMEM((16 * PAIRS, WIDE), BF16),
            pltpu.VMEM((DEVICES * MSG, WIDE), BF16),
            pltpu.VMEM((GROUP, 2 * ROWS, WIDE), BF16),
            dma,
            dma((GROUP,)),
            dma,
            dma,
            dma((GROUP,)),
            dma((GROUP,)),
            dma((2,)),
            dma((2,)),
            dma((GROUP,)),
            dma((GROUP,)),
            dma((2 * GROUP,)),
            dma((GROUP + 1,)),
            dma,
            dma((GROUP,)),
        ],
        compiler_params=pltpu.CompilerParams(
            collective_id=0, has_side_effects=True, vmem_limit_bytes=56 << 20
        ),
    )(segment_sums, lengths.reshape(1, ROWS), targets.reshape(1, ROWS), tile_masks.reshape(8))
    return losses.reshape(PAIRS), gradients


def solution(mesh):
    in_specs = (
        P(("blk", "dp"), None),
        P(("blk", "dp")),
        P(("blk", "dp")),
        P(("blk", "dp"), None, None, None),
    )
    out_specs = (P(("blk", "dp")), P(("blk", "dp"), None))
    return jax.shard_map(local, mesh=mesh, in_specs=in_specs, out_specs=out_specs, check_vma=False)
```

```python
import functools
import math

import jax
import jax.numpy as jnp
from jax import lax
from jax.experimental import pallas as pl
from jax.experimental.pallas import tpu as pltpu
from jax.sharding import PartitionSpec as P

MESH = pl.DeviceIdType.MESH
GROUP = 8
WIDE = 512
RINGS = 16
DEVICES = 128
ROWS = 128
PAIRS = 64
MSG = 16
F32 = jnp.float32
BF16 = jnp.bfloat16


def iota(shape, dim):
    return lax.broadcasted_iota(jnp.int32, shape, dim)


def nt_dot(a, b):
    return lax.dot_general(a, b, (((1,), (1,)), ((), ())), preferred_element_type=F32)


def tn_dot(a, b):
    return lax.dot_general(a, b, (((0,), (0,)), ((), ())), preferred_element_type=F32)


def nn_dot(a, b):
    return jnp.dot(a, b, preferred_element_type=F32)


def one_hot(mask):
    return jnp.where(mask, 1.0, 0.0).astype(BF16)


def place(part, ring):
    return (ring // 4) * 8 + part, ring % 4


def kernel(
    factor,
    coefficient,
    sums_hbm,
    lengths_ref,
    targets_ref,
    masks_ref,
    loss_ref,
    returned,
    back_one_hot,
    sums_ref,
    send_one_hot,
    sent,
    landed,
    meta_out,
    meta,
    codes,
    place_one_hot,
    return_one_hot,
    inverse,
    placed,
    queries,
    documents,
    partial,
    gathered,
    weights,
    totals,
    gradients,
    returning,
    load_sem,
    send_sem,
    land_sem,
    meta_send_sem,
    meta_sem,
    spread_send_sem,
    spread_sem,
    side_send_sem,
    side_sem,
    score_send_sem,
    score_sem,
    weight_send_sem,
    weight_sem,
    back_send_sem,
    back_sem,
):
    blk = lax.axis_index("blk")
    dp = lax.axis_index("dp")
    part = lax.rem(blk, 8)
    ring = (blk // 8) * 4 + dp
    x, y = lax.rem(blk, 16) // 4, lax.rem(blk, 4)
    z, core = (dp // 2) * 2 + blk // 16, lax.rem(dp, 2)
    own_sum = lax.rem(x + y + z, 4)
    me = (own_sum * 2 + core) * 16 + x * 4 + y
    xs = [lax.rem(x + i, 4) for i in range(4)]
    ys = [lax.rem(y + j, 4) for j in range(4)]

    def class_peers(turn, to_core):
        zs = [lax.rem(z + turn + 4 - m, 4) for m in range(4)]
        zs = [lax.rem(v, 2) * 8 + (v // 2) * 2 + to_core for v in zs]
        for i in range(4):
            for j in range(4):
                yield (
                    lax.rem(xs[i], 2) * 4 + ys[j],
                    (xs[i] // 2) * 4 + zs[(i + j) % 4],
                    xs[i] * 4 + ys[j],
                )

    def remote(src, dst, send, recv, to_part, to_ring):
        return pltpu.make_async_remote_copy(
            src_ref=src,
            dst_ref=dst,
            send_sem=send,
            recv_sem=recv,
            device_id=place(to_part, to_ring),
            device_id_type=MESH,
        )

    barrier = pltpu.get_barrier_semaphore()

    load = pltpu.make_async_copy(sums_hbm, sums_ref, load_sem)
    load.start()

    def greet(k, g):
        pl.semaphore_signal(barrier, inc=1, device_id=place(k, g), device_id_type=MESH)

    def greet_part(step, carry):
        k = lax.rem(part + step, GROUP)
        for g in range(RINGS):
            greet(k, g)
        return carry

    for turn in range(1, RINGS):
        greet(part, lax.rem(ring + turn, RINGS))
    lax.fori_loop(1, GROUP, greet_part, 0)

    target = targets_ref[...]
    length = lengths_ref[...].astype(F32)
    shard = target // ROWS
    slot = target % ROWS
    block = shard // 4
    to_ring = (block // 8) * 4 + shard % 4
    of_shard = one_hot(iota((DEVICES, ROWS), 0) == shard)
    earlier = one_hot(iota((ROWS, ROWS), 0) < iota((ROWS, ROWS), 1))
    before = nn_dot(of_shard, earlier)
    rank = jnp.sum(before * of_shard.astype(F32), axis=0, keepdims=True).astype(jnp.int32)
    inner = (block % 8) * 2 + rank
    position = to_ring * MSG + inner
    send_one_hot[...] = one_hot(iota((2 * ROWS, ROWS), 0) == position)
    column = jnp.transpose(jnp.broadcast_to(position.astype(F32), (ROWS, ROWS))).astype(jnp.int32)
    lanes = iota((ROWS, ROWS), 1)
    back_one_hot[:, :ROWS] = one_hot(column == lanes)
    back_one_hot[:, ROWS:] = one_hot(column == lanes + ROWS)
    code = ((slot % 2) * PAIRS + slot // 2 + 1).astype(F32)
    mine = iota((RINGS, ROWS), 0) == to_ring
    spot = one_hot(iota((ROWS, ROWS), 0) == part * MSG + inner)
    code_rows = nt_dot(jnp.where(mine, code, 0.0).astype(BF16), spot)
    length_rows = nt_dot(jnp.where(mine, length, 0.0).astype(BF16), spot)
    for g in range(RINGS):
        meta_out[g, 0:1, :] = code_rows[g : g + 1]
        meta_out[g, 1:2, :] = length_rows[g : g + 1]
    scale = 1.0 / jnp.transpose(jnp.broadcast_to(length, (ROWS, ROWS)))
    scale = jnp.concatenate([scale] * (WIDE // ROWS), axis=1)

    def pack(k):
        columns = sums_ref[:, k * WIDE : (k + 1) * WIDE].astype(F32)
        embedded = (columns * scale).astype(BF16)
        sent[k] = nn_dot(send_one_hot[...], embedded).astype(BF16)

    load.wait()
    for k in range(GROUP):
        pack(k)

    pl.semaphore_wait(barrier, DEVICES - 1)

    meta_dst = meta.at[part, me // 8]
    pltpu.make_async_copy(meta_out.at[ring], meta_dst, meta_sem).start()
    for turn in range(1, RINGS):
        g = lax.rem(ring + turn, RINGS)
        remote(meta_out.at[g], meta_dst, meta_send_sem, meta_sem, part, g).start()

    land_dst = landed.at[pl.ds(pl.multiple_of(me * MSG, MSG), MSG)]

    own_class = own_sum * 2 + core

    def sent_rows(k, g):
        return sent.at[k, pl.ds(pl.multiple_of(g * MSG, MSG), MSG)]

    def rows_out(step, carry):
        turn, to_core = lax.rem(step, 4), step // 4
        for index, (k, g, _) in enumerate(class_peers(turn, to_core)):
            if index == 0:
                stays = (turn == 0) & (to_core == core)

                @pl.when(stays)
                def _():
                    pltpu.make_async_copy(sent_rows(k, g), land_dst, land_sem.at[own_class]).start()

                @pl.when(jnp.logical_not(stays))
                def _():
                    remote(sent_rows(k, g), land_dst, send_sem, land_sem.at[own_class], k, g).start()

            else:
                remote(sent_rows(k, g), land_dst, send_sem, land_sem.at[own_class], k, g).start()
        return carry

    rows_out(0, 0)

    pltpu.make_async_copy(meta.at[part], meta.at[part], meta_sem).wait()

    def spread(step, carry):
        k = (part + step) % GROUP
        remote(
            meta.at[part], meta.at[part], spread_send_sem.at[step], spread_sem.at[part], k, ring
        ).start()
        return carry

    lax.fori_loop(1, GROUP, spread, 0)

    lax.fori_loop(1, 8, rows_out, 0)

    def spread_wait(step, carry):
        k = (part + GROUP - step) % GROUP
        remote(
            meta.at[k], meta.at[k], spread_send_sem.at[step], spread_sem.at[k], k, ring
        ).wait_recv()
        return carry

    lax.fori_loop(1, GROUP, spread_wait, 0)
    both = meta[0]
    for k in range(1, GROUP):
        both = both + meta[k]
    codes[...] = both

    inner_shard = (iota((1, ROWS), 1) % MSG) // 2

    def build(a, total):
        pair = codes[a]
        raw = pair[0:1].astype(jnp.int32) - 1
        live = jnp.where(raw >= PAIRS, 7 * PAIRS + raw, raw) + inner_shard * PAIRS
        full = jnp.where(raw >= 0, live, -1)
        matrix = one_hot(iota((8 * ROWS, ROWS), 0) == full)
        place_one_hot[a] = matrix
        down = jnp.transpose(jnp.broadcast_to(full.astype(F32), (ROWS, ROWS))).astype(jnp.int32)
        for s in range(GROUP):
            return_one_hot[pl.ds(pl.multiple_of(a * ROWS, ROWS), ROWS), s * ROWS : (s + 1) * ROWS] = (
                one_hot(down == lanes + s * ROWS)
            )
        wide = jnp.broadcast_to(pair[1:2], (ROWS, ROWS)).astype(BF16)
        inverse[...] = jnp.where(a == 0, 0.0, inverse[...]) + nt_dot(matrix, wide)
        return total

    inverse[...] = jnp.zeros(inverse.shape, F32)
    lax.fori_loop(0, 16, build, 0)
    inverse[...] = coefficient / inverse[...]

    after = (ring + 4) % RINGS
    ahead = (ring + 12) % RINGS
    to_next = remote(
        documents.at[8 * PAIRS :], documents.at[:PAIRS], side_send_sem.at[0], side_sem.at[0], part, after
    )
    to_last = remote(
        queries.at[:PAIRS], queries.at[8 * PAIRS :], side_send_sem.at[1], side_sem.at[1], part, ahead
    )

    def land(step):
        k = lax.rem(own_sum + 4 - step // 2, 4) * 2 + lax.rem(step, 2)
        rows = pl.ds(pl.multiple_of(k * 256, 256), 256)
        pltpu.make_async_copy(landed.at[rows], landed.at[rows], land_sem.at[k]).wait()
        return k, rows

    def put(step, block):
        k, rows = step
        slots = pl.ds(block * 256, 256)
        matrix = jnp.concatenate([place_one_hot[2 * k, slots], place_one_hot[2 * k + 1, slots]], axis=1)
        return nn_dot(matrix, landed[rows])

    def put_all(step, carry):
        now = land(step)
        for block in range(4):
            slots = pl.ds(block * 256, 256)
            placed[slots] = jnp.where(step == 0, 0.0, placed[slots]) + put(now, block)
        return carry

    placed[...] = jnp.zeros(placed.shape, F32)
    lax.fori_loop(0, GROUP - 1, put_all, 0)
    last = land(GROUP - 1)
    documents[320:576] = (placed[768:1024] + put(last, 3)).astype(BF16)
    to_next.start()
    queries[0:256] = (placed[0:256] + put(last, 0)).astype(BF16)
    to_last.start()
    queries[256:512] = (placed[256:512] + put(last, 1)).astype(BF16)
    documents[64:320] = (placed[512:768] + put(last, 2)).astype(BF16)

    def score(s):
        start = pl.multiple_of(s * PAIRS, PAIRS)
        value = nt_dot(queries[pl.ds(start, PAIRS)], documents[pl.ds(start, 2 * PAIRS)])

        @pl.when(s == part)
        def _():
            gathered[part] = value

        @pl.when(s != part)
        def _():
            partial[s] = value
            remote(
                partial.at[s], gathered.at[part], score_send_sem.at[s], score_sem.at[part], s, ring
            ).start()

    def score_step(step, carry):
        score(1 + lax.rem(part + step, GROUP - 1))
        return carry

    lax.fori_loop(0, GROUP - 1, score_step, 0)
    to_next.wait_recv()
    score(0)

    def score_wait(step, carry):
        k = (part + GROUP - step) % GROUP
        remote(
            partial.at[k], gathered.at[k], score_send_sem.at[k], score_sem.at[k], k, ring
        ).wait_recv()
        return carry

    lax.fori_loop(1, GROUP, score_wait, 0)
    scores = gathered[0]
    for k in range(1, GROUP):
        scores = scores + gathered[k]
    scores = factor * scores

    row = iota((PAIRS, 2 * PAIRS), 0)
    col = iota((PAIRS, 2 * PAIRS), 1)

    def tile(stop, i, j):
        return masks_ref[0, stop, i, j]

    top = jnp.where(
        col < 32,
        tile(1, 0, 0),
        jnp.where(col < 64, tile(1, 0, 1), jnp.where(col < 96, 1, tile(0, 0, 1))),
    )
    low = jnp.where(
        col < 32,
        tile(1, 1, 0),
        jnp.where(col < 64, tile(1, 1, 1), jnp.where(col < 96, tile(0, 1, 0), 1)),
    )
    live = jnp.where(row < 32, top, low) > 0
    masked = jnp.where(live, scores, -jnp.inf)
    highest = jnp.max(masked, axis=1, keepdims=True)
    log_total = highest + jnp.log(jnp.sum(jnp.exp(masked - highest), axis=1, keepdims=True))
    diagonal = jnp.sum(jnp.where(col == row + PAIRS, scores, 0.0), axis=1, keepdims=True)
    losses = jnp.where(col == row, log_total - diagonal, 0.0)
    loss_ref[...] = jnp.sum(losses, axis=0, keepdims=True)[:, :PAIRS]
    weights[part] = jnp.exp(masked - log_total).astype(BF16)

    def weight_out(step, carry):
        s = (part + step) % GROUP
        remote(
            weights.at[part], weights.at[part], weight_send_sem.at[step], weight_sem.at[part], s, ring
        ).start()
        return carry

    lax.fori_loop(1, GROUP, weight_out, 0)

    @pl.when(part == 0)
    def _():
        def far_out(step, carry):
            remote(
                weights.at[0], weights.at[8], weight_send_sem.at[8 + step], weight_sem.at[8], step, ahead
            ).start()
            return carry

        lax.fori_loop(0, GROUP, far_out, 0)

    def weight_wait(step, carry):
        k = (part + GROUP - step) % GROUP
        remote(
            weights.at[k], weights.at[k], weight_send_sem.at[step], weight_sem.at[k], k, ring
        ).wait_recv()
        return carry

    lax.fori_loop(1, GROUP, weight_wait, 0)
    remote(weights.at[0], weights.at[8], weight_send_sem.at[8], weight_sem.at[8], 0, ahead).wait_recv()
    to_last.wait_recv()

    def spread_scale(value):
        return jnp.concatenate([value] * (WIDE // ROWS), axis=1)

    def gradient(s, carry):
        start = pl.multiple_of(s * PAIRS, PAIRS)
        one = pl.ds(start, PAIRS)
        after_one = pl.ds(pl.multiple_of(s * PAIRS + PAIRS, PAIRS), PAIRS)
        two = pl.ds(start, 2 * PAIRS)
        weight = weights[s]
        term = nn_dot(weight, documents[two]) - documents[after_one].astype(F32)
        gradients[one] = (term * spread_scale(inverse[one])).astype(BF16)
        far = tn_dot(weight, queries[one])
        totals[one] = totals[one] + far[:PAIRS]
        totals[after_one] = far[PAIRS:] - queries[one].astype(F32)
        return carry

    totals[:PAIRS] = jnp.zeros((PAIRS, WIDE), F32)
    lax.fori_loop(0, GROUP, gradient, 0)
    totals[8 * PAIRS :] = totals[8 * PAIRS :] + tn_dot(weights[8], queries[8 * PAIRS :])[:PAIRS]
    gradients[8 * PAIRS :] = (totals[PAIRS:] * spread_scale(inverse[8 * PAIRS :])).astype(BF16)

    back_dst = returned.at[part, pl.ds(pl.multiple_of(ring * MSG, MSG), MSG)]

    def back_rows(label, spot):
        return returning.at[pl.ds(pl.multiple_of((label * 16 + spot) * MSG, MSG), MSG)]

    def rows_back(step, carry):
        turn, to_core = lax.rem(step, 4), step // 4
        label = lax.rem(own_sum + turn, 4) * 2 + to_core
        rows = pl.ds(pl.multiple_of(label * 256, 256), 256)
        returning[rows] = nn_dot(return_one_hot[rows], gradients[...]).astype(BF16)
        for index, (k, g, spot) in enumerate(class_peers(turn, to_core)):
            src = back_rows(label, spot)
            if index == 0:
                stays = (turn == 0) & (to_core == core)

                @pl.when(stays)
                def _():
                    pltpu.make_async_copy(src, back_dst, back_sem.at[part]).start()

                @pl.when(jnp.logical_not(stays))
                def _():
                    remote(src, back_dst, back_send_sem, back_sem.at[part], k, g).start()

            else:
                remote(src, back_dst, back_send_sem, back_sem.at[part], k, g).start()
        return carry

    lax.fori_loop(0, 8, rows_back, 0)

    def finish(step, carry):
        k = lax.rem(part + GROUP - step, GROUP)
        pltpu.make_async_copy(returned.at[k], returned.at[k], back_sem.at[k]).wait()
        return carry

    lax.fori_loop(0, GROUP, finish, 0)

    most = landed.at[pl.ds(0, (DEVICES - 1) * MSG)]
    pltpu.make_async_copy(most, most, send_sem).wait()
    pltpu.make_async_copy(most, most, back_send_sem).wait()

    fifteen = meta_out.at[pl.ds(0, RINGS - 1)]
    pltpu.make_async_copy(fifteen, fifteen, meta_send_sem).wait()
    to_next.wait_send()
    to_last.wait_send()

    def sent_wait(step, carry):
        k = (part + step) % GROUP
        remote(
            meta.at[part], meta.at[part], spread_send_sem.at[step], spread_sem.at[part], k, ring
        ).wait_send()
        remote(
            partial.at[k], gathered.at[part], score_send_sem.at[k], score_sem.at[part], k, ring
        ).wait_send()
        remote(
            weights.at[part], weights.at[part], weight_send_sem.at[step], weight_sem.at[part], k, ring
        ).wait_send()
        return carry

    lax.fori_loop(1, GROUP, sent_wait, 0)

    @pl.when(part == 0)
    def _():
        def far_wait(step, carry):
            remote(
                weights.at[0], weights.at[8], weight_send_sem.at[8 + step], weight_sem.at[8], step, ahead
            ).wait_send()
            return carry

        lax.fori_loop(0, GROUP, far_wait, 0)


def finish_kernel(loss_in, returned, back_one_hot, loss_ref, out_ref):
    loss_ref[...] = loss_in[...]
    for k in range(GROUP):
        out_ref[:, k * WIDE : (k + 1) * WIDE] = nn_dot(back_one_hot[...], returned[k]).astype(BF16)


def local(segment_sums, lengths, targets, tile_masks):
    width = segment_sums.shape[1]
    factor = 16.0 / math.sqrt(width)
    coefficient = factor / (PAIRS * DEVICES)
    vmem = pl.BlockSpec(memory_space=pltpu.VMEM)
    smem = pl.BlockSpec(memory_space=pltpu.SMEM)
    dma = pltpu.SemaphoreType.DMA
    results = pl.pallas_call(
        functools.partial(kernel, factor, coefficient),
        out_shape=(
            jax.ShapeDtypeStruct((1, PAIRS), F32),
            jax.ShapeDtypeStruct((GROUP, 2 * ROWS, WIDE), BF16),
            jax.ShapeDtypeStruct((ROWS, 2 * ROWS), BF16),
        ),
        in_specs=[pl.BlockSpec(memory_space=pl.ANY), vmem, vmem, smem],
        out_specs=(vmem, vmem, vmem),
        scratch_shapes=[
            pltpu.VMEM((ROWS, width), BF16),
            pltpu.VMEM((2 * ROWS, ROWS), BF16),
            pltpu.VMEM((GROUP, 2 * ROWS, WIDE), BF16),
            pltpu.VMEM((DEVICES * MSG, WIDE), BF16),
            pltpu.VMEM((RINGS, 2, ROWS), F32),
            pltpu.VMEM((GROUP, 16, 2, ROWS), F32),
            pltpu.VMEM((16, 2, ROWS), F32),
            pltpu.VMEM((16, GROUP * ROWS, ROWS), BF16),
            pltpu.VMEM((DEVICES * MSG, GROUP * ROWS), BF16),
            pltpu.VMEM((GROUP * ROWS, ROWS), F32),
            pltpu.VMEM((16 * PAIRS, WIDE), F32),
            pltpu.VMEM((9 * PAIRS, WIDE), BF16),
            pltpu.VMEM((9 * PAIRS, WIDE), BF16),
            pltpu.VMEM((GROUP, PAIRS, 2 * PAIRS), F32),
            pltpu.VMEM((GROUP, PAIRS, 2 * PAIRS), F32),
            pltpu.VMEM((9, PAIRS, 2 * PAIRS), BF16),
            pltpu.VMEM((9 * PAIRS, WIDE), F32),
            pltpu.VMEM((16 * PAIRS, WIDE), BF16),
            pltpu.VMEM((DEVICES * MSG, WIDE), BF16),
            dma,
            dma,
            dma((GROUP,)),
            dma,
            dma,
            dma((GROUP,)),
            dma((GROUP,)),
            dma((2,)),
            dma((2,)),
            dma((GROUP,)),
            dma((GROUP,)),
            dma((2 * GROUP,)),
            dma((GROUP + 1,)),
            dma,
            dma((GROUP,)),
        ],
        compiler_params=pltpu.CompilerParams(
            collective_id=0, has_side_effects=True, vmem_limit_bytes=56 << 20
        ),
    )(segment_sums, lengths.reshape(1, ROWS), targets.reshape(1, ROWS), tile_masks)
    losses, gradients = pl.pallas_call(
        finish_kernel,
        out_shape=(
            jax.ShapeDtypeStruct((1, PAIRS), F32),
            jax.ShapeDtypeStruct((ROWS, width), BF16),
        ),
        in_specs=[vmem, vmem, vmem],
        out_specs=(vmem, vmem),
    )(*results)
    return losses.reshape(PAIRS), gradients


def solution(mesh):
    in_specs = (
        P(("blk", "dp"), None),
        P(("blk", "dp")),
        P(("blk", "dp")),
        P(("blk", "dp"), None, None, None),
    )
    out_specs = (P(("blk", "dp")), P(("blk", "dp"), None))
    return jax.shard_map(local, mesh=mesh, in_specs=in_specs, out_specs=out_specs, check_vma=False)
```

```python
import functools
import math

import jax
import jax.numpy as jnp
from jax import lax
from jax.experimental import pallas as pl
from jax.experimental.pallas import tpu as pltpu
from jax.sharding import PartitionSpec as P

MESH = pl.DeviceIdType.MESH
GROUP = 8
WIDE = 512
RINGS = 16
DEVICES = 128
ROWS = 128
PAIRS = 64
MSG = 16
F32 = jnp.float32
BF16 = jnp.bfloat16


def iota(shape, dim):
    return lax.broadcasted_iota(jnp.int32, shape, dim)


def nt_dot(a, b):
    return lax.dot_general(a, b, (((1,), (1,)), ((), ())), preferred_element_type=F32)


def tn_dot(a, b):
    return lax.dot_general(a, b, (((0,), (0,)), ((), ())), preferred_element_type=F32)


def nn_dot(a, b):
    return jnp.dot(a, b, preferred_element_type=F32)


def one_hot(mask):
    return jnp.where(mask, 1.0, 0.0).astype(BF16)


def place(part, ring):
    return (lax.rem(ring, 8) // 2) * 8 + part, lax.rem(ring, 2) * 2 + ring // 8


def kernel(
    factor,
    coefficient,
    sums_hbm,
    lengths_ref,
    targets_ref,
    masks_ref,
    loss_ref,
    returned,
    back_one_hot,
    sums_ref,
    send_one_hot,
    sent,
    relay,
    landed,
    meta_out,
    meta,
    codes,
    place_one_hot,
    return_one_hot,
    inverse,
    placed,
    queries,
    documents,
    partial,
    gathered,
    weights,
    gradients,
    returning,
    load_sem,
    send_sem,
    land_sem,
    meta_send_sem,
    meta_sem,
    spread_send_sem,
    spread_sem,
    side_send_sem,
    side_sem,
    score_send_sem,
    score_sem,
    weight_send_sem,
    weight_sem,
    back_send_sem,
    back_sem,
    relay_send_sem,
    relay_sem,
):
    blk = lax.axis_index("blk")
    dp = lax.axis_index("dp")
    part = lax.rem(blk, 8)
    ring = lax.rem(dp, 2) * 8 + (blk // 8) * 2 + dp // 2
    x, y = lax.rem(blk, 16) // 4, lax.rem(blk, 4)
    z, core = (dp // 2) * 2 + blk // 16, lax.rem(dp, 2)
    own_sum = lax.rem(x + y + z, 4)
    me = (own_sum * 2 + core) * 16 + x * 4 + y
    xs = [lax.rem(x + i, 4) for i in range(4)]
    ys = [lax.rem(y + j, 4) for j in range(4)]

    def class_peers(turn, to_core):
        zs = [lax.rem(z + turn + 4 - m, 4) for m in range(4)]
        zs = [lax.rem(v, 2) * 4 + v // 2 + to_core * 8 for v in zs]
        for i in range(4):
            for j in range(4):
                yield (
                    lax.rem(xs[i], 2) * 4 + ys[j],
                    (xs[i] // 2) * 2 + zs[(i + j) % 4],
                    xs[i] * 4 + ys[j],
                )

    def remote(src, dst, send, recv, to_part, to_ring):
        return pltpu.make_async_remote_copy(
            src_ref=src,
            dst_ref=dst,
            send_sem=send,
            recv_sem=recv,
            device_id=place(to_part, to_ring),
            device_id_type=MESH,
        )

    barrier = pltpu.get_barrier_semaphore()

    load = pltpu.make_async_copy(sums_hbm, sums_ref, load_sem)
    load.start()

    def greet(k, g):
        pl.semaphore_signal(barrier, inc=1, device_id=place(k, g), device_id_type=MESH)

    def greet_part(step, carry):
        k = lax.rem(part + step, GROUP)
        for g in range(RINGS):
            greet(k, g)
        return carry

    for turn in range(1, RINGS):
        greet(part, lax.rem(ring + turn, RINGS))
    lax.fori_loop(1, GROUP, greet_part, 0)

    target = targets_ref[...]
    length = lengths_ref[...].astype(F32)
    shard = target // ROWS
    slot = target % ROWS
    block = shard // 4
    to_ring = (shard % 2) * 8 + (block // 8) * 2 + (shard % 4) // 2
    of_shard = one_hot(iota((DEVICES, ROWS), 0) == shard)
    earlier = one_hot(iota((ROWS, ROWS), 0) < iota((ROWS, ROWS), 1))
    before = nn_dot(of_shard, earlier)
    rank = jnp.sum(before * of_shard.astype(F32), axis=0, keepdims=True).astype(jnp.int32)
    inner = (block % 8) * 2 + rank
    position = to_ring * MSG + inner
    send_one_hot[...] = one_hot(iota((2 * ROWS, ROWS), 0) == position)
    column = jnp.transpose(jnp.broadcast_to(position.astype(F32), (ROWS, ROWS))).astype(jnp.int32)
    lanes = iota((ROWS, ROWS), 1)
    back_one_hot[:, :ROWS] = one_hot(column == lanes)
    back_one_hot[:, ROWS:] = one_hot(column == lanes + ROWS)
    code = ((slot % 2) * PAIRS + slot // 2 + 1).astype(F32)
    mine = iota((RINGS, ROWS), 0) == to_ring
    spot = one_hot(iota((ROWS, ROWS), 0) == part * MSG + inner)
    code_rows = nt_dot(jnp.where(mine, code, 0.0).astype(BF16), spot)
    length_rows = nt_dot(jnp.where(mine, length, 0.0).astype(BF16), spot)
    for g in range(RINGS):
        meta_out[g, 0:1, :] = code_rows[g : g + 1]
        meta_out[g, 1:2, :] = length_rows[g : g + 1]
    scale = 1.0 / jnp.transpose(jnp.broadcast_to(length, (ROWS, ROWS)))
    scale = jnp.concatenate([scale] * (WIDE // ROWS), axis=1)

    def pack(k):
        columns = sums_ref[:, k * WIDE : (k + 1) * WIDE].astype(F32)
        embedded = (columns * scale).astype(BF16)
        sent[k] = nn_dot(send_one_hot[...], embedded).astype(BF16)

    load.wait()
    for k in range(GROUP):
        pack(k)

    pl.semaphore_wait(barrier, DEVICES - 1)

    meta_dst = meta.at[part, me // 8]
    pltpu.make_async_copy(meta_out.at[ring], meta_dst, meta_sem).start()
    for turn in range(1, RINGS):
        g = lax.rem(ring + turn, RINGS)
        remote(meta_out.at[g], meta_dst, meta_send_sem, meta_sem, part, g).start()

    land_dst = landed.at[pl.ds(pl.multiple_of(me * MSG, MSG), MSG)]

    mate_dst = landed.at[pl.ds(pl.multiple_of((me - core * 16) * MSG, MSG), MSG)]
    hand_over = pltpu.make_async_remote_copy(
        src_ref=sent.at[:, pl.ds(ROWS, ROWS)],
        dst_ref=relay,
        send_sem=relay_send_sem.at[0],
        recv_sem=relay_sem,
        device_id=(blk, (dp // 2) * 2 + 1 - core),
        device_id_type=MESH,
    )

    def send_class(turn, to_core, source, dst, sem, stays):
        for index, (k, g, _) in enumerate(class_peers(turn, to_core)):
            src = source(k, g)
            if index == 0:

                @pl.when(stays)
                def _():
                    pltpu.make_async_copy(src, dst, land_sem.at[own_sum]).start()

                @pl.when(jnp.logical_not(stays))
                def _():
                    remote(src, dst, sem, land_sem.at[own_sum], k, g).start()

            else:
                remote(src, dst, sem, land_sem.at[own_sum], k, g).start()

    def sent_rows(k, g):
        return sent.at[k, pl.ds(pl.multiple_of(g * MSG, MSG), MSG)]

    def relay_rows(k, g):
        return relay.at[k, pl.ds(pl.multiple_of((g - GROUP) * MSG, MSG), MSG)]

    def rows_out(turn, carry):
        send_class(turn, 0, sent_rows, land_dst, send_sem, (turn == 0) & (core == 0))
        return carry

    def rows_on(turn, carry):
        send_class(turn, 1, sent_rows, land_dst, send_sem, turn == 0)
        send_class(turn, 1, relay_rows, mate_dst, relay_send_sem.at[1], turn == 0)
        return carry

    lax.fori_loop(0, 2, rows_out, 0)

    @pl.when(core == 0)
    def _():
        hand_over.start()

    pltpu.make_async_copy(meta.at[part], meta.at[part], meta_sem).wait()

    others = [lax.rem(part + step, GROUP) for step in range(1, GROUP)]
    for k in others:
        remote(meta.at[part], meta.at[part], spread_send_sem, spread_sem, k, ring).start()

    lax.fori_loop(2, 4, rows_out, 0)

    @pl.when(core == 1)
    def _():
        hand_over.wait_recv()
        lax.fori_loop(0, 4, rows_on, 0)

    seven_meta = meta.at[pl.ds(0, GROUP - 1)]
    pltpu.make_async_copy(seven_meta, seven_meta, spread_sem).wait()
    both = meta[0]
    for k in range(1, GROUP):
        both = both + meta[k]
    codes[...] = both

    inner_shard = (iota((1, ROWS), 1) % MSG) // 2

    def full_slots(pair):
        raw = pair[0:1].astype(jnp.int32) - 1
        live = jnp.where(raw >= PAIRS, 7 * PAIRS + raw, raw) + inner_shard * PAIRS
        return jnp.where(raw >= 0, live, -1)

    def build(owners, carry):
        for q in range(4):
            full = full_slots(codes[4 * owners + q])
            place_one_hot[owners, :, q * ROWS : (q + 1) * ROWS] = one_hot(
                iota((8 * ROWS, ROWS), 0) == full
            )
        return carry

    lax.fori_loop(0, 4, build, 0)

    def build_return(a, carry):
        full = full_slots(codes[a]).astype(F32)
        down = jnp.transpose(jnp.broadcast_to(full, (ROWS, ROWS))).astype(jnp.int32)
        rows = pl.ds(pl.multiple_of(a * ROWS, ROWS), ROWS)
        for s in range(GROUP):
            return_one_hot[rows, s * ROWS : (s + 1) * ROWS] = one_hot(down == lanes + s * ROWS)
        return carry

    def build_inverse(block, carry):
        rows = pl.ds(pl.multiple_of(block * 256, 256), 256)
        total = None
        for owners in range(4):
            wide = jnp.concatenate([codes[4 * owners + q][1:2] for q in range(4)], axis=1)
            wide = jnp.broadcast_to(wide, (ROWS, 4 * ROWS)).astype(BF16)
            term = nt_dot(place_one_hot[owners, rows], wide)
            total = term if total is None else total + term
        inverse[rows] = coefficient / total
        return carry

    lax.fori_loop(0, 16, build_return, 0)
    lax.fori_loop(0, 4, build_inverse, 0)

    after = core * 8 + lax.rem(lax.rem(ring, 8) + 2, 8)
    ahead = core * 8 + lax.rem(lax.rem(ring, 8) + 6, 8)
    to_next = remote(
        documents.at[8 * PAIRS :], documents.at[:PAIRS], side_send_sem.at[0], side_sem.at[0], part, after
    )
    to_last = remote(
        queries.at[:PAIRS], queries.at[8 * PAIRS :], side_send_sem.at[1], side_sem.at[1], part, ahead
    )

    def land(step):
        owners = lax.rem(own_sum + 4 - step, 4)
        rows = pl.ds(pl.multiple_of(owners * 512, 512), 512)
        pltpu.make_async_copy(landed.at[rows], landed.at[rows], land_sem.at[owners]).wait()
        return owners, rows

    def put(now, block):
        owners, rows = now
        return nn_dot(place_one_hot[owners, block * 256 : (block + 1) * 256], landed[rows])

    first = land(0)
    for block in range(4):
        placed[block * 256 : (block + 1) * 256] = put(first, block)

    def put_more(step, carry):
        now = land(step)
        for block in range(4):
            slots = pl.ds(block * 256, 256)
            placed[slots] = placed[slots] + put(now, block)
        return carry

    lax.fori_loop(1, 3, put_more, 0)
    last = land(3)
    documents[320:576] = (placed[768:1024] + put(last, 3)).astype(BF16)
    to_next.start()
    queries[0:256] = (placed[0:256] + put(last, 0)).astype(BF16)
    to_last.start()
    queries[256:512] = (placed[256:512] + put(last, 1)).astype(BF16)
    documents[64:320] = (placed[512:768] + put(last, 2)).astype(BF16)

    def score(s):
        return nt_dot(
            queries[s * PAIRS : (s + 1) * PAIRS], documents[s * PAIRS : (s + 2) * PAIRS]
        )

    def score_out(s):
        return remote(
            partial.at[s], gathered.at[part], score_send_sem, score_sem, s, ring
        )

    for s in range(1, GROUP):
        partial[s] = score(s)
    for s in others:

        @pl.when(s != 0)
        def _():
            score_out(s).start()

    to_next.wait_recv()
    partial[0] = score(0)

    @pl.when(part != 0)
    def _():
        score_out(0).start()

    gathered[part] = partial[part]

    row = iota((PAIRS, 2 * PAIRS), 0)
    col = iota((PAIRS, 2 * PAIRS), 1)

    def tile(stop, i, j):
        return masks_ref[0, stop, i, j]

    top = jnp.where(
        col < 32,
        tile(1, 0, 0),
        jnp.where(col < 64, tile(1, 0, 1), jnp.where(col < 96, 1, tile(0, 0, 1))),
    )
    low = jnp.where(
        col < 32,
        tile(1, 1, 0),
        jnp.where(col < 64, tile(1, 1, 1), jnp.where(col < 96, tile(0, 1, 0), 1)),
    )
    live = jnp.where(row < 32, top, low) > 0
    seven_scores = gathered.at[pl.ds(0, GROUP - 1)]
    pltpu.make_async_copy(seven_scores, seven_scores, score_sem).wait()
    scores = gathered[0]
    for k in range(1, GROUP):
        scores = scores + gathered[k]
    scores = factor * scores

    masked = jnp.where(live, scores, -jnp.inf)
    highest = jnp.max(masked, axis=1, keepdims=True)
    log_total = highest + jnp.log(jnp.sum(jnp.exp(masked - highest), axis=1, keepdims=True))
    weights[part] = jnp.exp(masked - log_total).astype(BF16)

    for k in others:
        remote(weights.at[part], weights.at[part], weight_send_sem, weight_sem, k, ring).start()

    @pl.when(part == 0)
    def _():
        for k in range(GROUP):
            remote(weights.at[0], weights.at[8], weight_send_sem, weight_sem, k, ahead).start()

    diagonal = jnp.sum(jnp.where(col == row + PAIRS, scores, 0.0), axis=1, keepdims=True)
    losses = jnp.where(col == row, log_total - diagonal, 0.0)
    loss_ref[...] = jnp.sum(losses, axis=0, keepdims=True)[:, :PAIRS]
    eight_weights = weights.at[pl.ds(0, GROUP)]
    pltpu.make_async_copy(eight_weights, eight_weights, weight_sem).wait()
    to_last.wait_recv()

    def spread_scale(value):
        return jnp.concatenate([value] * (WIDE // ROWS), axis=1)

    def rows_of(s):
        return slice(s * PAIRS, (s + 1) * PAIRS)

    held = None
    for s in range(GROUP + 1):
        weight = weights[s]
        far = tn_dot(weight, queries[rows_of(s)])
        if s > 0:
            slots = rows_of(GROUP + s - 1)
            gradients[slots] = ((held + far[:PAIRS]) * spread_scale(inverse[slots])).astype(BF16)
        if s < GROUP:
            held = far[PAIRS:] - queries[rows_of(s)].astype(F32)
            own = rows_of(s)
            term = nn_dot(weight, documents[s * PAIRS : (s + 2) * PAIRS])
            term = term - documents[rows_of(s + 1)].astype(F32)
            gradients[own] = (term * spread_scale(inverse[own])).astype(BF16)

    back_dst = returned.at[part, pl.ds(pl.multiple_of(ring * MSG, MSG), MSG)]

    def back_rows(label, spot):
        return returning.at[pl.ds(pl.multiple_of((label * 16 + spot) * MSG, MSG), MSG)]

    def rows_back(step, carry):
        turn, to_core = lax.rem(step, 4), step // 4
        label = lax.rem(own_sum + turn, 4) * 2 + to_core
        rows = pl.ds(pl.multiple_of(label * 256, 256), 256)
        returning[rows] = nn_dot(return_one_hot[rows], gradients[...]).astype(BF16)
        for index, (k, g, spot) in enumerate(class_peers(turn, to_core)):
            src = back_rows(label, spot)
            if index == 0:
                stays = (turn == 0) & (to_core == core)

                @pl.when(stays)
                def _():
                    pltpu.make_async_copy(src, back_dst, back_sem.at[part]).start()

                @pl.when(jnp.logical_not(stays))
                def _():
                    remote(src, back_dst, back_send_sem, back_sem.at[part], k, g).start()

            else:
                remote(src, back_dst, back_send_sem, back_sem.at[part], k, g).start()
        return carry

    lax.fori_loop(0, 8, rows_back, 0)

    def finish(step, carry):
        k = lax.rem(part + GROUP - step, GROUP)
        pltpu.make_async_copy(returned.at[k], returned.at[k], back_sem.at[k]).wait()
        return carry

    lax.fori_loop(0, GROUP, finish, 0)

    most = landed.at[pl.ds(0, (DEVICES - 1) * MSG)]
    half = landed.at[pl.ds(0, (PAIRS - 1) * MSG)]

    @pl.when(core == 0)
    def _():
        hand_over.wait_send()
        pltpu.make_async_copy(half, half, send_sem).wait()

    @pl.when(core == 1)
    def _():
        pltpu.make_async_copy(most, most, send_sem).wait()
        pltpu.make_async_copy(half, half, relay_send_sem.at[1]).wait()

    pltpu.make_async_copy(most, most, back_send_sem).wait()
    fifteen = meta_out.at[pl.ds(0, RINGS - 1)]
    pltpu.make_async_copy(fifteen, fifteen, meta_send_sem).wait()
    to_next.wait_send()
    to_last.wait_send()

    pltpu.make_async_copy(seven_meta, seven_meta, spread_send_sem).wait()
    pltpu.make_async_copy(seven_scores, seven_scores, score_send_sem).wait()
    seven_weights = weights.at[pl.ds(0, GROUP - 1)]
    pltpu.make_async_copy(seven_weights, seven_weights, weight_send_sem).wait()

    @pl.when(part == 0)
    def _():
        pltpu.make_async_copy(eight_weights, eight_weights, weight_send_sem).wait()


def finish_kernel(loss_in, returned, back_one_hot, loss_ref, out_ref):
    loss_ref[...] = loss_in[...]
    for k in range(GROUP):
        out_ref[:, k * WIDE : (k + 1) * WIDE] = nn_dot(back_one_hot[...], returned[k]).astype(BF16)


def local(segment_sums, lengths, targets, tile_masks):
    width = segment_sums.shape[1]
    factor = 16.0 / math.sqrt(width)
    coefficient = factor / (PAIRS * DEVICES)
    vmem = pl.BlockSpec(memory_space=pltpu.VMEM)
    smem = pl.BlockSpec(memory_space=pltpu.SMEM)
    dma = pltpu.SemaphoreType.DMA
    results = pl.pallas_call(
        functools.partial(kernel, factor, coefficient),
        out_shape=(
            jax.ShapeDtypeStruct((1, PAIRS), F32),
            jax.ShapeDtypeStruct((GROUP, 2 * ROWS, WIDE), BF16),
            jax.ShapeDtypeStruct((ROWS, 2 * ROWS), BF16),
        ),
        in_specs=[pl.BlockSpec(memory_space=pl.ANY), vmem, vmem, smem],
        out_specs=(vmem, vmem, vmem),
        scratch_shapes=[
            pltpu.VMEM((ROWS, width), BF16),
            pltpu.VMEM((2 * ROWS, ROWS), BF16),
            pltpu.VMEM((GROUP, 2 * ROWS, WIDE), BF16),
            pltpu.VMEM((GROUP, ROWS, WIDE), BF16),
            pltpu.VMEM((DEVICES * MSG, WIDE), BF16),
            pltpu.VMEM((RINGS, 2, ROWS), F32),
            pltpu.VMEM((GROUP, 16, 2, ROWS), F32),
            pltpu.VMEM((16, 2, ROWS), F32),
            pltpu.VMEM((4, GROUP * ROWS, 4 * ROWS), BF16),
            pltpu.VMEM((DEVICES * MSG, GROUP * ROWS), BF16),
            pltpu.VMEM((GROUP * ROWS, ROWS), F32),
            pltpu.VMEM((16 * PAIRS, WIDE), F32),
            pltpu.VMEM((9 * PAIRS, WIDE), BF16),
            pltpu.VMEM((9 * PAIRS, WIDE), BF16),
            pltpu.VMEM((GROUP, PAIRS, 2 * PAIRS), F32),
            pltpu.VMEM((GROUP, PAIRS, 2 * PAIRS), F32),
            pltpu.VMEM((9, PAIRS, 2 * PAIRS), BF16),
            pltpu.VMEM((16 * PAIRS, WIDE), BF16),
            pltpu.VMEM((DEVICES * MSG, WIDE), BF16),
            dma,
            dma,
            dma((4,)),
            dma,
            dma,
            dma,
            dma,
            dma((2,)),
            dma((2,)),
            dma,
            dma,
            dma,
            dma,
            dma,
            dma((GROUP,)),
            dma((2,)),
            dma,
        ],
        compiler_params=pltpu.CompilerParams(
            collective_id=0, has_side_effects=True, vmem_limit_bytes=56 << 20
        ),
    )(segment_sums, lengths.reshape(1, ROWS), targets.reshape(1, ROWS), tile_masks)
    losses, gradients = pl.pallas_call(
        finish_kernel,
        out_shape=(
            jax.ShapeDtypeStruct((1, PAIRS), F32),
            jax.ShapeDtypeStruct((ROWS, width), BF16),
        ),
        in_specs=[vmem, vmem, vmem],
        out_specs=(vmem, vmem),
    )(*results)
    return losses.reshape(PAIRS), gradients


def solution(mesh):
    in_specs = (
        P(("blk", "dp"), None),
        P(("blk", "dp")),
        P(("blk", "dp")),
        P(("blk", "dp"), None, None, None),
    )
    out_specs = (P(("blk", "dp")), P(("blk", "dp"), None))
    return jax.shard_map(local, mesh=mesh, in_specs=in_specs, out_specs=out_specs, check_vma=False)
```

```python
import functools
import math

import jax
import jax.numpy as jnp
from jax import lax
from jax.experimental import pallas as pl
from jax.experimental.pallas import tpu as pltpu
from jax.sharding import PartitionSpec as P

MESH = pl.DeviceIdType.MESH
GROUP = 8
WIDE = 512
RINGS = 16
DEVICES = 128
ROWS = 128
PAIRS = 64
MSG = 16
F32 = jnp.float32
BF16 = jnp.bfloat16


def iota(shape, dim):
    return lax.broadcasted_iota(jnp.int32, shape, dim)


def nt_dot(a, b):
    return lax.dot_general(a, b, (((1,), (1,)), ((), ())), preferred_element_type=F32)


def tn_dot(a, b):
    return lax.dot_general(a, b, (((0,), (0,)), ((), ())), preferred_element_type=F32)


def nn_dot(a, b):
    return jnp.dot(a, b, preferred_element_type=F32)


def one_hot(mask):
    return jnp.where(mask, 1.0, 0.0).astype(BF16)


def mirror(part, group):
    return lax.rem(part // 4 + group, 2) * 4 + lax.rem(part, 4)


def place(part, ring):
    group = lax.rem(ring, 8) // 2
    return group * 8 + mirror(part, group), lax.rem(ring, 2) * 2 + ring // 8


def kernel(
    factor,
    coefficient,
    sums_hbm,
    lengths_ref,
    targets_ref,
    masks_ref,
    loss_ref,
    returned,
    back_one_hot,
    sums_ref,
    send_one_hot,
    sent,
    relay,
    landed,
    meta_out,
    meta,
    codes,
    place_one_hot,
    return_one_hot,
    inverse,
    placed,
    queries,
    documents,
    partial,
    gathered,
    weights,
    gradients,
    returning,
    load_sem,
    send_sem,
    land_sem,
    meta_send_sem,
    meta_sem,
    spread_send_sem,
    spread_sem,
    side_send_sem,
    side_sem,
    score_send_sem,
    score_sem,
    weight_send_sem,
    weight_sem,
    back_send_sem,
    back_sem,
    relay_send_sem,
    relay_sem,
):
    blk = lax.axis_index("blk")
    dp = lax.axis_index("dp")
    home = lax.rem(blk, 8)
    part = mirror(home, blk // 8)
    ring = lax.rem(dp, 2) * 8 + (blk // 8) * 2 + dp // 2
    x, y = lax.rem(blk, 16) // 4, lax.rem(blk, 4)
    z, core = (dp // 2) * 2 + blk // 16, lax.rem(dp, 2)
    own_sum = lax.rem(x + y + z, 4)
    me = (own_sum * 2 + core) * 16 + x * 4 + y
    xs = [lax.rem(x + i, 4) for i in range(4)]
    ys = [lax.rem(y + j, 4) for j in range(4)]

    def class_peers(turn, to_core):
        zs = [lax.rem(z + turn + 4 - m, 4) for m in range(4)]
        zs = [lax.rem(v, 2) * 4 + v // 2 + to_core * 8 for v in zs]
        for i in range(4):
            for j in range(4):
                yield (
                    lax.rem(xs[i] + xs[i] // 2, 2) * 4 + ys[j],
                    (xs[i] // 2) * 2 + zs[(i + j) % 4],
                    xs[i] * 4 + ys[j],
                )

    def remote(src, dst, send, recv, to_part, to_ring):
        return pltpu.make_async_remote_copy(
            src_ref=src,
            dst_ref=dst,
            send_sem=send,
            recv_sem=recv,
            device_id=place(to_part, to_ring),
            device_id_type=MESH,
        )

    barrier = pltpu.get_barrier_semaphore()

    load = pltpu.make_async_copy(sums_hbm, sums_ref, load_sem)
    load.start()

    def greet(k, g):
        pl.semaphore_signal(barrier, inc=1, device_id=place(k, g), device_id_type=MESH)

    def greet_part(step, carry):
        k = lax.rem(part + step, GROUP)
        for g in range(RINGS):
            greet(k, g)
        return carry

    for turn in range(1, RINGS):
        greet(part, lax.rem(ring + turn, RINGS))
    lax.fori_loop(1, GROUP, greet_part, 0)

    target = targets_ref[...]
    length = lengths_ref[...].astype(F32)
    shard = target // ROWS
    slot = target % ROWS
    block = shard // 4
    to_ring = (shard % 2) * 8 + (block // 8) * 2 + (shard % 4) // 2
    of_shard = one_hot(iota((DEVICES, ROWS), 0) == shard)
    earlier = one_hot(iota((ROWS, ROWS), 0) < iota((ROWS, ROWS), 1))
    before = nn_dot(of_shard, earlier)
    rank = jnp.sum(before * of_shard.astype(F32), axis=0, keepdims=True).astype(jnp.int32)
    inner = (block % 8) * 2 + rank
    position = to_ring * MSG + inner
    send_one_hot[...] = one_hot(iota((2 * ROWS, ROWS), 0) == position)
    column = jnp.transpose(jnp.broadcast_to(position.astype(F32), (ROWS, ROWS))).astype(jnp.int32)
    lanes = iota((ROWS, ROWS), 1)
    back_one_hot[:, :ROWS] = one_hot(column == lanes)
    back_one_hot[:, ROWS:] = one_hot(column == lanes + ROWS)
    code = ((slot % 2) * PAIRS + slot // 2 + 1).astype(F32)
    mine = iota((RINGS, ROWS), 0) == to_ring
    spot = one_hot(iota((ROWS, ROWS), 0) == home * MSG + inner)
    code_rows = nt_dot(jnp.where(mine, code, 0.0).astype(BF16), spot)
    length_rows = nt_dot(jnp.where(mine, length, 0.0).astype(BF16), spot)
    for g in range(RINGS):
        meta_out[g, 0:1, :] = code_rows[g : g + 1]
        meta_out[g, 1:2, :] = length_rows[g : g + 1]
    scale = 1.0 / jnp.transpose(jnp.broadcast_to(length, (ROWS, ROWS)))
    scale = jnp.concatenate([scale] * (WIDE // ROWS), axis=1)

    def pack(k):
        columns = sums_ref[:, k * WIDE : (k + 1) * WIDE].astype(F32)
        embedded = (columns * scale).astype(BF16)
        sent[k] = nn_dot(send_one_hot[...], embedded).astype(BF16)

    load.wait()
    for k in range(GROUP):
        pack(k)

    pl.semaphore_wait(barrier, DEVICES - 1)

    meta_dst = meta.at[part, me // 8]
    pltpu.make_async_copy(meta_out.at[ring], meta_dst, meta_sem).start()
    for turn in range(1, RINGS):
        g = lax.rem(ring + turn, RINGS)
        remote(meta_out.at[g], meta_dst, meta_send_sem, meta_sem, part, g).start()

    land_dst = landed.at[pl.ds(pl.multiple_of(me * MSG, MSG), MSG)]

    mate_dst = landed.at[pl.ds(pl.multiple_of((me - core * 16) * MSG, MSG), MSG)]
    hand_over = pltpu.make_async_remote_copy(
        src_ref=sent.at[:, pl.ds(ROWS, ROWS)],
        dst_ref=relay,
        send_sem=relay_send_sem.at[0],
        recv_sem=relay_sem,
        device_id=(blk, (dp // 2) * 2 + 1 - core),
        device_id_type=MESH,
    )

    def send_class(turn, to_core, source, dst, sem, stays):
        for index, (k, g, _) in enumerate(class_peers(turn, to_core)):
            src = source(k, g)
            if index == 0:

                @pl.when(stays)
                def _():
                    pltpu.make_async_copy(src, dst, land_sem.at[own_sum]).start()

                @pl.when(jnp.logical_not(stays))
                def _():
                    remote(src, dst, sem, land_sem.at[own_sum], k, g).start()

            else:
                remote(src, dst, sem, land_sem.at[own_sum], k, g).start()

    def sent_rows(k, g):
        return sent.at[k, pl.ds(pl.multiple_of(g * MSG, MSG), MSG)]

    def relay_rows(k, g):
        return relay.at[k, pl.ds(pl.multiple_of((g - GROUP) * MSG, MSG), MSG)]

    def rows_out(turn, carry):
        send_class(turn, 0, sent_rows, land_dst, send_sem, (turn == 0) & (core == 0))
        return carry

    def rows_on(turn, carry):
        send_class(turn, 1, sent_rows, land_dst, send_sem, turn == 0)
        send_class(turn, 1, relay_rows, mate_dst, relay_send_sem.at[1], turn == 0)
        return carry

    lax.fori_loop(0, 2, rows_out, 0)

    @pl.when(core == 0)
    def _():
        hand_over.start()

    pltpu.make_async_copy(meta.at[part], meta.at[part], meta_sem).wait()

    others = [lax.rem(part + step, GROUP) for step in range(1, GROUP)]
    for k in others:
        remote(meta.at[part], meta.at[part], spread_send_sem, spread_sem, k, ring).start()

    lax.fori_loop(2, 4, rows_out, 0)

    @pl.when(core == 1)
    def _():
        hand_over.wait_recv()
        lax.fori_loop(0, 4, rows_on, 0)

    seven_meta = meta.at[pl.ds(0, GROUP - 1)]
    pltpu.make_async_copy(seven_meta, seven_meta, spread_sem).wait()
    both = meta[0]
    for k in range(1, GROUP):
        both = both + meta[k]
    codes[...] = both

    inner_shard = (iota((1, ROWS), 1) % MSG) // 2

    def full_slots(pair):
        raw = pair[0:1].astype(jnp.int32) - 1
        live = jnp.where(raw >= PAIRS, 7 * PAIRS + raw, raw) + inner_shard * PAIRS
        return jnp.where(raw >= 0, live, -1)

    def build(owners, carry):
        for q in range(4):
            full = full_slots(codes[4 * owners + q])
            place_one_hot[owners, :, q * ROWS : (q + 1) * ROWS] = one_hot(
                iota((8 * ROWS, ROWS), 0) == full
            )
        return carry

    lax.fori_loop(0, 4, build, 0)

    def build_return(a, carry):
        full = full_slots(codes[a]).astype(F32)
        down = jnp.transpose(jnp.broadcast_to(full, (ROWS, ROWS))).astype(jnp.int32)
        rows = pl.ds(pl.multiple_of(a * ROWS, ROWS), ROWS)
        for s in range(GROUP):
            return_one_hot[rows, s * ROWS : (s + 1) * ROWS] = one_hot(down == lanes + s * ROWS)
        return carry

    def build_inverse(block, carry):
        rows = pl.ds(pl.multiple_of(block * 256, 256), 256)
        total = None
        for owners in range(4):
            wide = jnp.concatenate([codes[4 * owners + q][1:2] for q in range(4)], axis=1)
            wide = jnp.broadcast_to(wide, (ROWS, 4 * ROWS)).astype(BF16)
            term = nt_dot(place_one_hot[owners, rows], wide)
            total = term if total is None else total + term
        inverse[rows] = coefficient / total
        return carry

    lax.fori_loop(0, 16, build_return, 0)
    lax.fori_loop(0, 4, build_inverse, 0)

    after = core * 8 + lax.rem(lax.rem(ring, 8) + 2, 8)
    ahead = core * 8 + lax.rem(lax.rem(ring, 8) + 6, 8)
    to_next = remote(
        documents.at[8 * PAIRS :], documents.at[:PAIRS], side_send_sem.at[0], side_sem.at[0], part, after
    )
    to_last = remote(
        queries.at[:PAIRS], queries.at[8 * PAIRS :], side_send_sem.at[1], side_sem.at[1], part, ahead
    )

    def land(step):
        owners = lax.rem(own_sum + 4 - step, 4)
        rows = pl.ds(pl.multiple_of(owners * 512, 512), 512)
        pltpu.make_async_copy(landed.at[rows], landed.at[rows], land_sem.at[owners]).wait()
        return owners, rows

    def put(now, block):
        owners, rows = now
        return nn_dot(place_one_hot[owners, block * 256 : (block + 1) * 256], landed[rows])

    first = land(0)
    for block in range(4):
        placed[block * 256 : (block + 1) * 256] = put(first, block)

    def put_more(step, carry):
        now = land(step)
        for block in range(4):
            slots = pl.ds(block * 256, 256)
            placed[slots] = placed[slots] + put(now, block)
        return carry

    lax.fori_loop(1, 3, put_more, 0)
    last = land(3)
    documents[320:576] = (placed[768:1024] + put(last, 3)).astype(BF16)
    to_next.start()
    queries[0:256] = (placed[0:256] + put(last, 0)).astype(BF16)
    to_last.start()
    queries[256:512] = (placed[256:512] + put(last, 1)).astype(BF16)
    documents[64:320] = (placed[512:768] + put(last, 2)).astype(BF16)

    def score(s):
        return nt_dot(
            queries[s * PAIRS : (s + 1) * PAIRS], documents[s * PAIRS : (s + 2) * PAIRS]
        )

    def score_out(s):
        return remote(
            partial.at[s],
            gathered.at[part],
            score_send_sem,
            score_sem,
            mirror(s, blk // 8),
            ring,
        )

    for s in range(1, GROUP):
        partial[s] = score(s)
    for k in others:
        s = mirror(k, blk // 8)

        @pl.when(s != 0)
        def _():
            score_out(s).start()

    to_next.wait_recv()
    partial[0] = score(0)

    @pl.when(home != 0)
    def _():
        score_out(0).start()

    gathered[part] = partial[home]

    row = iota((PAIRS, 2 * PAIRS), 0)
    col = iota((PAIRS, 2 * PAIRS), 1)

    def tile(stop, i, j):
        return masks_ref[0, stop, i, j]

    top = jnp.where(
        col < 32,
        tile(1, 0, 0),
        jnp.where(col < 64, tile(1, 0, 1), jnp.where(col < 96, 1, tile(0, 0, 1))),
    )
    low = jnp.where(
        col < 32,
        tile(1, 1, 0),
        jnp.where(col < 64, tile(1, 1, 1), jnp.where(col < 96, tile(0, 1, 0), 1)),
    )
    live = jnp.where(row < 32, top, low) > 0
    seven_scores = gathered.at[pl.ds(0, GROUP - 1)]
    pltpu.make_async_copy(seven_scores, seven_scores, score_sem).wait()
    scores = gathered[0]
    for k in range(1, GROUP):
        scores = scores + gathered[k]
    scores = factor * scores

    masked = jnp.where(live, scores, -jnp.inf)
    highest = jnp.max(masked, axis=1, keepdims=True)
    log_total = highest + jnp.log(jnp.sum(jnp.exp(masked - highest), axis=1, keepdims=True))
    weights[home] = jnp.exp(masked - log_total).astype(BF16)

    @pl.when(home == 0)
    def _():
        for k in range(GROUP):
            remote(weights.at[0], weights.at[8], weight_send_sem, weight_sem, k, ahead).start()

    for k in others:
        remote(weights.at[home], weights.at[home], weight_send_sem, weight_sem, k, ring).start()

    diagonal = jnp.sum(jnp.where(col == row + PAIRS, scores, 0.0), axis=1, keepdims=True)
    losses = jnp.where(col == row, log_total - diagonal, 0.0)
    loss_ref[...] = jnp.sum(losses, axis=0, keepdims=True)[:, :PAIRS]
    eight_weights = weights.at[pl.ds(0, GROUP)]
    pltpu.make_async_copy(eight_weights, eight_weights, weight_sem).wait()
    to_last.wait_recv()

    def spread_scale(value):
        return jnp.concatenate([value] * (WIDE // ROWS), axis=1)

    def rows_of(s):
        return slice(s * PAIRS, (s + 1) * PAIRS)

    held = None
    for s in range(GROUP + 1):
        weight = weights[s]
        far = tn_dot(weight, queries[rows_of(s)])
        if s > 0:
            slots = rows_of(GROUP + s - 1)
            gradients[slots] = ((held + far[:PAIRS]) * spread_scale(inverse[slots])).astype(BF16)
        if s < GROUP:
            held = far[PAIRS:] - queries[rows_of(s)].astype(F32)
            own = rows_of(s)
            term = nn_dot(weight, documents[s * PAIRS : (s + 2) * PAIRS])
            term = term - documents[rows_of(s + 1)].astype(F32)
            gradients[own] = (term * spread_scale(inverse[own])).astype(BF16)

    back_dst = returned.at[part, pl.ds(pl.multiple_of(ring * MSG, MSG), MSG)]

    def back_rows(label, spot):
        return returning.at[pl.ds(pl.multiple_of((label * 16 + spot) * MSG, MSG), MSG)]

    def rows_back(step, carry):
        turn, to_core = lax.rem(step, 4), lax.rem(step // 4 + core, 2)
        label = lax.rem(own_sum + turn, 4) * 2 + to_core
        rows = pl.ds(pl.multiple_of(label * 256, 256), 256)
        returning[rows] = nn_dot(return_one_hot[rows], gradients[...]).astype(BF16)
        for index, (k, g, spot) in enumerate(class_peers(turn, to_core)):
            src = back_rows(label, spot)
            if index == 0:
                stays = (turn == 0) & (to_core == core)

                @pl.when(stays)
                def _():
                    pltpu.make_async_copy(src, back_dst, back_sem.at[part]).start()

                @pl.when(jnp.logical_not(stays))
                def _():
                    remote(src, back_dst, back_send_sem, back_sem.at[part], k, g).start()

            else:
                remote(src, back_dst, back_send_sem, back_sem.at[part], k, g).start()
        return carry

    lax.fori_loop(0, 8, rows_back, 0)

    def finish(step, carry):
        k = lax.rem(part + GROUP - step, GROUP)
        pltpu.make_async_copy(returned.at[k], returned.at[k], back_sem.at[k]).wait()
        return carry

    lax.fori_loop(0, GROUP, finish, 0)

    most = landed.at[pl.ds(0, (DEVICES - 1) * MSG)]
    half = landed.at[pl.ds(0, (PAIRS - 1) * MSG)]

    @pl.when(core == 0)
    def _():
        hand_over.wait_send()
        pltpu.make_async_copy(half, half, send_sem).wait()

    @pl.when(core == 1)
    def _():
        pltpu.make_async_copy(most, most, send_sem).wait()
        pltpu.make_async_copy(half, half, relay_send_sem.at[1]).wait()

    pltpu.make_async_copy(most, most, back_send_sem).wait()
    fifteen = meta_out.at[pl.ds(0, RINGS - 1)]
    pltpu.make_async_copy(fifteen, fifteen, meta_send_sem).wait()
    to_next.wait_send()
    to_last.wait_send()

    pltpu.make_async_copy(seven_meta, seven_meta, spread_send_sem).wait()
    pltpu.make_async_copy(seven_scores, seven_scores, score_send_sem).wait()
    seven_weights = weights.at[pl.ds(0, GROUP - 1)]
    pltpu.make_async_copy(seven_weights, seven_weights, weight_send_sem).wait()

    @pl.when(home == 0)
    def _():
        pltpu.make_async_copy(eight_weights, eight_weights, weight_send_sem).wait()


def finish_kernel(loss_in, returned, back_one_hot, loss_ref, out_ref):
    loss_ref[...] = loss_in[...]
    for k in range(GROUP):
        out_ref[:, k * WIDE : (k + 1) * WIDE] = nn_dot(back_one_hot[...], returned[k]).astype(BF16)


def local(segment_sums, lengths, targets, tile_masks):
    width = segment_sums.shape[1]
    factor = 16.0 / math.sqrt(width)
    coefficient = factor / (PAIRS * DEVICES)
    vmem = pl.BlockSpec(memory_space=pltpu.VMEM)
    smem = pl.BlockSpec(memory_space=pltpu.SMEM)
    dma = pltpu.SemaphoreType.DMA
    results = pl.pallas_call(
        functools.partial(kernel, factor, coefficient),
        out_shape=(
            jax.ShapeDtypeStruct((1, PAIRS), F32),
            jax.ShapeDtypeStruct((GROUP, 2 * ROWS, WIDE), BF16),
            jax.ShapeDtypeStruct((ROWS, 2 * ROWS), BF16),
        ),
        in_specs=[pl.BlockSpec(memory_space=pl.ANY), vmem, vmem, smem],
        out_specs=(vmem, vmem, vmem),
        scratch_shapes=[
            pltpu.VMEM((ROWS, width), BF16),
            pltpu.VMEM((2 * ROWS, ROWS), BF16),
            pltpu.VMEM((GROUP, 2 * ROWS, WIDE), BF16),
            pltpu.VMEM((GROUP, ROWS, WIDE), BF16),
            pltpu.VMEM((DEVICES * MSG, WIDE), BF16),
            pltpu.VMEM((RINGS, 2, ROWS), F32),
            pltpu.VMEM((GROUP, 16, 2, ROWS), F32),
            pltpu.VMEM((16, 2, ROWS), F32),
            pltpu.VMEM((4, GROUP * ROWS, 4 * ROWS), BF16),
            pltpu.VMEM((DEVICES * MSG, GROUP * ROWS), BF16),
            pltpu.VMEM((GROUP * ROWS, ROWS), F32),
            pltpu.VMEM((16 * PAIRS, WIDE), F32),
            pltpu.VMEM((9 * PAIRS, WIDE), BF16),
            pltpu.VMEM((9 * PAIRS, WIDE), BF16),
            pltpu.VMEM((GROUP, PAIRS, 2 * PAIRS), F32),
            pltpu.VMEM((GROUP, PAIRS, 2 * PAIRS), F32),
            pltpu.VMEM((9, PAIRS, 2 * PAIRS), BF16),
            pltpu.VMEM((16 * PAIRS, WIDE), BF16),
            pltpu.VMEM((DEVICES * MSG, WIDE), BF16),
            dma,
            dma,
            dma((4,)),
            dma,
            dma,
            dma,
            dma,
            dma((2,)),
            dma((2,)),
            dma,
            dma,
            dma,
            dma,
            dma,
            dma((GROUP,)),
            dma((2,)),
            dma,
        ],
        compiler_params=pltpu.CompilerParams(
            collective_id=0, has_side_effects=True, vmem_limit_bytes=56 << 20
        ),
    )(segment_sums, lengths.reshape(1, ROWS), targets.reshape(1, ROWS), tile_masks)
    losses, gradients = pl.pallas_call(
        finish_kernel,
        out_shape=(
            jax.ShapeDtypeStruct((1, PAIRS), F32),
            jax.ShapeDtypeStruct((ROWS, width), BF16),
        ),
        in_specs=[vmem, vmem, vmem],
        out_specs=(vmem, vmem),
    )(*results)
    return losses.reshape(PAIRS), gradients


def solution(mesh):
    in_specs = (
        P(("blk", "dp"), None),
        P(("blk", "dp")),
        P(("blk", "dp")),
        P(("blk", "dp"), None, None, None),
    )
    out_specs = (P(("blk", "dp")), P(("blk", "dp"), None))
    return jax.shard_map(local, mesh=mesh, in_specs=in_specs, out_specs=out_specs, check_vma=False)
```

```python
import functools
import math

import jax
import jax.numpy as jnp
from jax import lax
from jax.experimental import pallas as pl
from jax.experimental.pallas import tpu as pltpu
from jax.sharding import PartitionSpec as P

MESH = pl.DeviceIdType.MESH
GROUP = 8
WIDE = 512
RINGS = 16
DEVICES = 128
ROWS = 128
PAIRS = 64
MSG = 16
F32 = jnp.float32
BF16 = jnp.bfloat16


def iota(shape, dim):
    return lax.broadcasted_iota(jnp.int32, shape, dim)


def nt_dot(a, b):
    return lax.dot_general(a, b, (((1,), (1,)), ((), ())), preferred_element_type=F32)


def tn_dot(a, b):
    return lax.dot_general(a, b, (((0,), (0,)), ((), ())), preferred_element_type=F32)


def nn_dot(a, b):
    return jnp.dot(a, b, preferred_element_type=F32)


def one_hot(mask):
    return jnp.where(mask, 1.0, 0.0).astype(BF16)


def mirror(part, group):
    return lax.rem(part // 4 + group, 2) * 4 + lax.rem(part, 4)


def place(part, ring):
    group = lax.rem(ring, 8) // 2
    return group * 8 + mirror(part, group), lax.rem(ring, 2) * 2 + ring // 8


def kernel(
    factor,
    coefficient,
    sums_hbm,
    lengths_ref,
    targets_ref,
    masks_ref,
    loss_ref,
    returned,
    back_one_hot,
    sums_ref,
    send_one_hot,
    sent,
    relay,
    landed,
    meta_out,
    meta,
    codes,
    place_one_hot,
    return_one_hot,
    inverse,
    placed,
    queries,
    documents,
    partial,
    gathered,
    weights,
    gradients,
    returning,
    load_sem,
    send_sem,
    land_sem,
    meta_send_sem,
    meta_sem,
    spread_send_sem,
    spread_sem,
    side_send_sem,
    side_sem,
    score_send_sem,
    score_sem,
    weight_send_sem,
    weight_sem,
    far_send_sem,
    far_sem,
    back_send_sem,
    back_sem,
    relay_send_sem,
    relay_sem,
):
    blk = lax.axis_index("blk")
    dp = lax.axis_index("dp")
    home = lax.rem(blk, 8)
    part = mirror(home, blk // 8)
    ring = lax.rem(dp, 2) * 8 + (blk // 8) * 2 + dp // 2
    x, y = lax.rem(blk, 16) // 4, lax.rem(blk, 4)
    z, core = (dp // 2) * 2 + blk // 16, lax.rem(dp, 2)
    own_sum = lax.rem(x + y + z, 4)
    me = (own_sum * 2 + core) * 16 + x * 4 + y
    xs = [lax.rem(x + i, 4) for i in range(4)]
    ys = [lax.rem(y + j, 4) for j in range(4)]

    def class_peers(turn, to_core):
        zs = [lax.rem(z + turn + 4 - m, 4) for m in range(4)]
        zs = [lax.rem(v, 2) * 4 + v // 2 + to_core * 8 for v in zs]
        for i in range(4):
            for j in range(4):
                yield (
                    lax.rem(xs[i] + xs[i] // 2, 2) * 4 + ys[j],
                    (xs[i] // 2) * 2 + zs[(i + j) % 4],
                    xs[i] * 4 + ys[j],
                )

    def remote(src, dst, send, recv, to_part, to_ring):
        return pltpu.make_async_remote_copy(
            src_ref=src,
            dst_ref=dst,
            send_sem=send,
            recv_sem=recv,
            device_id=place(to_part, to_ring),
            device_id_type=MESH,
        )

    barrier = pltpu.get_barrier_semaphore()

    load = pltpu.make_async_copy(sums_hbm, sums_ref, load_sem)
    load.start()

    def greet(k, g):
        pl.semaphore_signal(barrier, inc=1, device_id=place(k, g), device_id_type=MESH)

    def greet_part(step, carry):
        k = lax.rem(part + step, GROUP)
        for g in range(RINGS):
            greet(k, g)
        return carry

    for turn in range(1, RINGS):
        greet(part, lax.rem(ring + turn, RINGS))
    lax.fori_loop(1, GROUP, greet_part, 0)

    target = targets_ref[...]
    length = lengths_ref[...].astype(F32)
    shard = target // ROWS
    slot = target % ROWS
    block = shard // 4
    to_ring = (shard % 2) * 8 + (block // 8) * 2 + (shard % 4) // 2
    of_shard = one_hot(iota((DEVICES, ROWS), 0) == shard)
    earlier = one_hot(iota((ROWS, ROWS), 0) < iota((ROWS, ROWS), 1))
    before = nn_dot(of_shard, earlier)
    rank = jnp.sum(before * of_shard.astype(F32), axis=0, keepdims=True).astype(jnp.int32)
    inner = (block % 8) * 2 + rank
    position = to_ring * MSG + inner
    send_one_hot[...] = one_hot(iota((2 * ROWS, ROWS), 0) == position)
    column = jnp.transpose(jnp.broadcast_to(position.astype(F32), (ROWS, ROWS))).astype(jnp.int32)
    lanes = iota((ROWS, ROWS), 1)
    back_one_hot[:, :ROWS] = one_hot(column == lanes)
    back_one_hot[:, ROWS:] = one_hot(column == lanes + ROWS)
    code = ((slot % 2) * PAIRS + slot // 2 + 1).astype(F32)
    mine = iota((RINGS, ROWS), 0) == to_ring
    spot = one_hot(iota((ROWS, ROWS), 0) == home * MSG + inner)
    code_rows = nt_dot(jnp.where(mine, code, 0.0).astype(BF16), spot)
    length_rows = nt_dot(jnp.where(mine, length, 0.0).astype(BF16), spot)
    for g in range(RINGS):
        meta_out[g, 0:1, :] = code_rows[g : g + 1]
        meta_out[g, 1:2, :] = length_rows[g : g + 1]
    scale = 1.0 / jnp.transpose(jnp.broadcast_to(length, (ROWS, ROWS)))
    scale = jnp.concatenate([scale] * (WIDE // ROWS), axis=1)

    def pack(k):
        columns = sums_ref[:, k * WIDE : (k + 1) * WIDE].astype(F32)
        embedded = (columns * scale).astype(BF16)
        sent[k] = nn_dot(send_one_hot[...], embedded).astype(BF16)

    load.wait()
    for k in range(GROUP):
        pack(k)

    pl.semaphore_wait(barrier, DEVICES - 1)

    meta_dst = meta.at[part, me // 8]
    pltpu.make_async_copy(meta_out.at[ring], meta_dst, meta_sem).start()
    for turn in range(1, RINGS):
        g = lax.rem(ring + turn, RINGS)
        remote(meta_out.at[g], meta_dst, meta_send_sem, meta_sem, part, g).start()

    land_dst = landed.at[pl.ds(pl.multiple_of(me * MSG, MSG), MSG)]

    mate_dst = landed.at[pl.ds(pl.multiple_of((me - core * 16) * MSG, MSG), MSG)]
    hand_over = pltpu.make_async_remote_copy(
        src_ref=sent.at[:, pl.ds(ROWS, ROWS)],
        dst_ref=relay,
        send_sem=relay_send_sem.at[0],
        recv_sem=relay_sem,
        device_id=(blk, (dp // 2) * 2 + 1 - core),
        device_id_type=MESH,
    )

    def send_class(turn, to_core, source, dst, sem, stays):
        for index, (k, g, _) in enumerate(class_peers(turn, to_core)):
            src = source(k, g)
            if index == 0:

                @pl.when(stays)
                def _():
                    pltpu.make_async_copy(src, dst, land_sem.at[own_sum]).start()

                @pl.when(jnp.logical_not(stays))
                def _():
                    remote(src, dst, sem, land_sem.at[own_sum], k, g).start()

            else:
                remote(src, dst, sem, land_sem.at[own_sum], k, g).start()

    def sent_rows(k, g):
        return sent.at[k, pl.ds(pl.multiple_of(g * MSG, MSG), MSG)]

    def relay_rows(k, g):
        return relay.at[k, pl.ds(pl.multiple_of((g - GROUP) * MSG, MSG), MSG)]

    def rows_out(turn, carry):
        send_class(turn, 0, sent_rows, land_dst, send_sem, (turn == 0) & (core == 0))
        return carry

    def rows_on(turn, carry):
        send_class(turn, 1, sent_rows, land_dst, send_sem, turn == 0)
        send_class(turn, 1, relay_rows, mate_dst, relay_send_sem.at[1], turn == 0)
        return carry

    lax.fori_loop(0, 2, rows_out, 0)

    @pl.when(core == 0)
    def _():
        hand_over.start()

    pltpu.make_async_copy(meta.at[part], meta.at[part], meta_sem).wait()

    others = [lax.rem(part + step, GROUP) for step in range(1, GROUP)]
    for k in others:
        remote(meta.at[part], meta.at[part], spread_send_sem, spread_sem, k, ring).start()

    lax.fori_loop(2, 4, rows_out, 0)

    @pl.when(core == 1)
    def _():
        hand_over.wait_recv()
        lax.fori_loop(0, 4, rows_on, 0)

    seven_meta = meta.at[pl.ds(0, GROUP - 1)]
    pltpu.make_async_copy(seven_meta, seven_meta, spread_sem).wait()
    both = meta[0]
    for k in range(1, GROUP):
        both = both + meta[k]
    codes[...] = both

    inner_shard = (iota((1, ROWS), 1) % MSG) // 2

    def full_slots(pair):
        raw = pair[0:1].astype(jnp.int32) - 1
        live = jnp.where(raw >= PAIRS, 7 * PAIRS + raw, raw) + inner_shard * PAIRS
        return jnp.where(raw >= 0, live, -1)

    def build(owners, carry):
        for q in range(4):
            full = full_slots(codes[4 * owners + q])
            place_one_hot[owners, :, q * ROWS : (q + 1) * ROWS] = one_hot(
                iota((8 * ROWS, ROWS), 0) == full
            )
        return carry

    lax.fori_loop(0, 4, build, 0)

    def build_return(a, carry):
        full = full_slots(codes[a]).astype(F32)
        down = jnp.transpose(jnp.broadcast_to(full, (ROWS, ROWS))).astype(jnp.int32)
        rows = pl.ds(pl.multiple_of(a * ROWS, ROWS), ROWS)
        for s in range(GROUP):
            return_one_hot[rows, s * ROWS : (s + 1) * ROWS] = one_hot(down == lanes + s * ROWS)
        return carry

    def build_inverse(block, carry):
        rows = pl.ds(pl.multiple_of(block * 256, 256), 256)
        total = None
        for owners in range(4):
            wide = jnp.concatenate([codes[4 * owners + q][1:2] for q in range(4)], axis=1)
            wide = jnp.broadcast_to(wide, (ROWS, 4 * ROWS)).astype(BF16)
            term = nt_dot(place_one_hot[owners, rows], wide)
            total = term if total is None else total + term
        inverse[rows] = coefficient / total
        return carry

    lax.fori_loop(0, 16, build_return, 0)
    lax.fori_loop(0, 4, build_inverse, 0)

    after = core * 8 + lax.rem(lax.rem(ring, 8) + 2, 8)
    ahead = core * 8 + lax.rem(lax.rem(ring, 8) + 6, 8)
    to_next = remote(
        documents.at[8 * PAIRS :], documents.at[:PAIRS], side_send_sem.at[0], side_sem.at[0], part, after
    )
    to_last = remote(
        queries.at[:PAIRS], queries.at[8 * PAIRS :], side_send_sem.at[1], side_sem.at[1], part, ahead
    )

    def land(step):
        owners = lax.rem(own_sum + 4 - step, 4)
        rows = pl.ds(pl.multiple_of(owners * 512, 512), 512)
        pltpu.make_async_copy(landed.at[rows], landed.at[rows], land_sem.at[owners]).wait()
        return owners, rows

    def put(now, block):
        owners, rows = now
        return nn_dot(place_one_hot[owners, block * 256 : (block + 1) * 256], landed[rows])

    first = land(0)
    for block in range(4):
        placed[block * 256 : (block + 1) * 256] = put(first, block)

    def put_more(step, carry):
        now = land(step)
        for block in range(4):
            slots = pl.ds(block * 256, 256)
            placed[slots] = placed[slots] + put(now, block)
        return carry

    lax.fori_loop(1, 3, put_more, 0)
    last = land(3)
    documents[320:576] = (placed[768:1024] + put(last, 3)).astype(BF16)
    to_next.start()
    queries[0:256] = (placed[0:256] + put(last, 0)).astype(BF16)
    to_last.start()
    queries[256:512] = (placed[256:512] + put(last, 1)).astype(BF16)
    documents[64:320] = (placed[512:768] + put(last, 2)).astype(BF16)

    def score(s):
        return nt_dot(
            queries[s * PAIRS : (s + 1) * PAIRS], documents[s * PAIRS : (s + 2) * PAIRS]
        )

    def score_out(s):
        return remote(
            partial.at[s],
            gathered.at[part],
            score_send_sem,
            score_sem,
            mirror(s, blk // 8),
            ring,
        )

    for s in range(1, GROUP):
        partial[s] = score(s)
    for k in others:
        s = mirror(k, blk // 8)

        @pl.when(s != 0)
        def _():
            score_out(s).start()

    to_next.wait_recv()
    partial[0] = score(0)

    @pl.when(home != 0)
    def _():
        score_out(0).start()

    gathered[part] = partial[home]

    row = iota((PAIRS, 2 * PAIRS), 0)
    col = iota((PAIRS, 2 * PAIRS), 1)

    def tile(stop, i, j):
        return masks_ref[0, stop, i, j]

    top = jnp.where(
        col < 32,
        tile(1, 0, 0),
        jnp.where(col < 64, tile(1, 0, 1), jnp.where(col < 96, 1, tile(0, 0, 1))),
    )
    low = jnp.where(
        col < 32,
        tile(1, 1, 0),
        jnp.where(col < 64, tile(1, 1, 1), jnp.where(col < 96, tile(0, 1, 0), 1)),
    )
    live = jnp.where(row < 32, top, low) > 0
    seven_scores = gathered.at[pl.ds(0, GROUP - 1)]
    pltpu.make_async_copy(seven_scores, seven_scores, score_sem).wait()
    scores = gathered[0]
    for k in range(1, GROUP):
        scores = scores + gathered[k]
    scores = factor * scores

    masked = jnp.where(live, scores, -jnp.inf)
    highest = jnp.max(masked, axis=1, keepdims=True)
    shares = jnp.exp(masked - highest)
    share_total = jnp.sum(shares, axis=1, keepdims=True)
    weights[home] = (shares * (1.0 / share_total)).astype(BF16)

    @pl.when(home == 0)
    def _():
        for k in range(GROUP):
            remote(weights.at[0], weights.at[8], far_send_sem, far_sem, k, ahead).start()

    for k in others:
        remote(weights.at[home], weights.at[home], weight_send_sem, weight_sem, k, ring).start()

    log_total = highest + jnp.log(share_total)
    diagonal = jnp.sum(jnp.where(col == row + PAIRS, scores, 0.0), axis=1, keepdims=True)
    losses = jnp.where(col == row, log_total - diagonal, 0.0)
    loss_ref[...] = jnp.sum(losses, axis=0, keepdims=True)[:, :PAIRS]
    seven_weights = weights.at[pl.ds(0, GROUP - 1)]
    pltpu.make_async_copy(seven_weights, seven_weights, weight_sem).wait()

    def spread_scale(value):
        return jnp.concatenate([value] * (WIDE // ROWS), axis=1)

    def rows_of(s):
        return slice(s * PAIRS, (s + 1) * PAIRS)

    held = None
    for s in range(GROUP + 1):
        if s == GROUP:
            to_last.wait_recv()
            pltpu.make_async_copy(weights.at[s], weights.at[s], far_sem).wait()
        weight = weights[s]
        far = tn_dot(weight, queries[rows_of(s)])
        if s > 0:
            slots = rows_of(GROUP + s - 1)
            gradients[slots] = ((held + far[:PAIRS]) * spread_scale(inverse[slots])).astype(BF16)
        if s < GROUP:
            held = far[PAIRS:] - queries[rows_of(s)].astype(F32)
            own = rows_of(s)
            term = nn_dot(weight, documents[s * PAIRS : (s + 2) * PAIRS])
            term = term - documents[rows_of(s + 1)].astype(F32)
            gradients[own] = (term * spread_scale(inverse[own])).astype(BF16)

    back_dst = returned.at[part, pl.ds(pl.multiple_of(ring * MSG, MSG), MSG)]

    def back_rows(label, spot):
        return returning.at[pl.ds(pl.multiple_of((label * 16 + spot) * MSG, MSG), MSG)]

    def rows_back(step, carry):
        turn, to_core = lax.rem(step, 4), lax.rem(step // 4 + core, 2)
        label = lax.rem(own_sum + turn, 4) * 2 + to_core
        rows = pl.ds(pl.multiple_of(label * 256, 256), 256)
        returning[rows] = nn_dot(return_one_hot[rows], gradients[...]).astype(BF16)
        for index, (k, g, spot) in enumerate(class_peers(turn, to_core)):
            src = back_rows(label, spot)
            if index == 0:
                stays = (turn == 0) & (to_core == core)

                @pl.when(stays)
                def _():
                    pltpu.make_async_copy(src, back_dst, back_sem.at[part]).start()

                @pl.when(jnp.logical_not(stays))
                def _():
                    remote(src, back_dst, back_send_sem, back_sem.at[part], k, g).start()

            else:
                remote(src, back_dst, back_send_sem, back_sem.at[part], k, g).start()
        return carry

    lax.fori_loop(0, 8, rows_back, 0)

    def finish(step, carry):
        k = lax.rem(part + GROUP - step, GROUP)
        pltpu.make_async_copy(returned.at[k], returned.at[k], back_sem.at[k]).wait()
        return carry

    lax.fori_loop(0, GROUP, finish, 0)

    most = landed.at[pl.ds(0, (DEVICES - 1) * MSG)]
    half = landed.at[pl.ds(0, (PAIRS - 1) * MSG)]

    @pl.when(core == 0)
    def _():
        hand_over.wait_send()
        pltpu.make_async_copy(half, half, send_sem).wait()

    @pl.when(core == 1)
    def _():
        pltpu.make_async_copy(most, most, send_sem).wait()
        pltpu.make_async_copy(half, half, relay_send_sem.at[1]).wait()

    pltpu.make_async_copy(most, most, back_send_sem).wait()
    fifteen = meta_out.at[pl.ds(0, RINGS - 1)]
    pltpu.make_async_copy(fifteen, fifteen, meta_send_sem).wait()
    to_next.wait_send()
    to_last.wait_send()

    pltpu.make_async_copy(seven_meta, seven_meta, spread_send_sem).wait()
    pltpu.make_async_copy(seven_scores, seven_scores, score_send_sem).wait()
    pltpu.make_async_copy(seven_weights, seven_weights, weight_send_sem).wait()

    @pl.when(home == 0)
    def _():
        eight_weights = weights.at[pl.ds(0, GROUP)]
        pltpu.make_async_copy(eight_weights, eight_weights, far_send_sem).wait()


def finish_kernel(loss_in, returned, back_one_hot, loss_ref, out_ref):
    loss_ref[...] = loss_in[...]
    for k in range(GROUP):
        out_ref[:, k * WIDE : (k + 1) * WIDE] = nn_dot(back_one_hot[...], returned[k]).astype(BF16)


def local(segment_sums, lengths, targets, tile_masks):
    width = segment_sums.shape[1]
    factor = 16.0 / math.sqrt(width)
    coefficient = factor / (PAIRS * DEVICES)
    vmem = pl.BlockSpec(memory_space=pltpu.VMEM)
    smem = pl.BlockSpec(memory_space=pltpu.SMEM)
    dma = pltpu.SemaphoreType.DMA
    results = pl.pallas_call(
        functools.partial(kernel, factor, coefficient),
        out_shape=(
            jax.ShapeDtypeStruct((1, PAIRS), F32),
            jax.ShapeDtypeStruct((GROUP, 2 * ROWS, WIDE), BF16),
            jax.ShapeDtypeStruct((ROWS, 2 * ROWS), BF16),
        ),
        in_specs=[pl.BlockSpec(memory_space=pl.ANY), vmem, vmem, smem],
        out_specs=(vmem, vmem, vmem),
        scratch_shapes=[
            pltpu.VMEM((ROWS, width), BF16),
            pltpu.VMEM((2 * ROWS, ROWS), BF16),
            pltpu.VMEM((GROUP, 2 * ROWS, WIDE), BF16),
            pltpu.VMEM((GROUP, ROWS, WIDE), BF16),
            pltpu.VMEM((DEVICES * MSG, WIDE), BF16),
            pltpu.VMEM((RINGS, 2, ROWS), F32),
            pltpu.VMEM((GROUP, 16, 2, ROWS), F32),
            pltpu.VMEM((16, 2, ROWS), F32),
            pltpu.VMEM((4, GROUP * ROWS, 4 * ROWS), BF16),
            pltpu.VMEM((DEVICES * MSG, GROUP * ROWS), BF16),
            pltpu.VMEM((GROUP * ROWS, ROWS), F32),
            pltpu.VMEM((16 * PAIRS, WIDE), F32),
            pltpu.VMEM((9 * PAIRS, WIDE), BF16),
            pltpu.VMEM((9 * PAIRS, WIDE), BF16),
            pltpu.VMEM((GROUP, PAIRS, 2 * PAIRS), F32),
            pltpu.VMEM((GROUP, PAIRS, 2 * PAIRS), F32),
            pltpu.VMEM((9, PAIRS, 2 * PAIRS), BF16),
            pltpu.VMEM((16 * PAIRS, WIDE), BF16),
            pltpu.VMEM((DEVICES * MSG, WIDE), BF16),
            dma,
            dma,
            dma((4,)),
            dma,
            dma,
            dma,
            dma,
            dma((2,)),
            dma((2,)),
            dma,
            dma,
            dma,
            dma,
            dma,
            dma,
            dma,
            dma((GROUP,)),
            dma((2,)),
            dma,
        ],
        compiler_params=pltpu.CompilerParams(
            collective_id=0, has_side_effects=True, vmem_limit_bytes=56 << 20
        ),
    )(segment_sums, lengths.reshape(1, ROWS), targets.reshape(1, ROWS), tile_masks)
    losses, gradients = pl.pallas_call(
        finish_kernel,
        out_shape=(
            jax.ShapeDtypeStruct((1, PAIRS), F32),
            jax.ShapeDtypeStruct((ROWS, width), BF16),
        ),
        in_specs=[vmem, vmem, vmem],
        out_specs=(vmem, vmem),
    )(*results)
    return losses.reshape(PAIRS), gradients


def solution(mesh):
    in_specs = (
        P(("blk", "dp"), None),
        P(("blk", "dp")),
        P(("blk", "dp")),
        P(("blk", "dp"), None, None, None),
    )
    out_specs = (P(("blk", "dp")), P(("blk", "dp"), None))
    return jax.shard_map(local, mesh=mesh, in_specs=in_specs, out_specs=out_specs, check_vma=False)
```

```python
import functools
import math

import jax
import jax.numpy as jnp
from jax import lax
from jax.experimental import pallas as pl
from jax.experimental.pallas import tpu as pltpu
from jax.sharding import PartitionSpec as P

MESH = pl.DeviceIdType.MESH
GROUP = 8
WIDE = 512
RINGS = 16
DEVICES = 128
ROWS = 128
PAIRS = 64
MSG = 16
F32 = jnp.float32
BF16 = jnp.bfloat16


def iota(shape, dim):
    return lax.broadcasted_iota(jnp.int32, shape, dim)


def nt_dot(a, b):
    return lax.dot_general(a, b, (((1,), (1,)), ((), ())), preferred_element_type=F32)


def tn_dot(a, b):
    return lax.dot_general(a, b, (((0,), (0,)), ((), ())), preferred_element_type=F32)


def nn_dot(a, b):
    return jnp.dot(a, b, preferred_element_type=F32)


def one_hot(mask):
    return jnp.where(mask, 1.0, 0.0).astype(BF16)


def mirror(part, group):
    return lax.rem(part // 4 + group, 2) * 4 + lax.rem(part, 4)


def place(part, ring):
    group = lax.rem(ring, 8) // 2
    return group * 8 + mirror(part, group), lax.rem(ring, 2) * 2 + ring // 8


def kernel(
    factor,
    coefficient,
    sums_hbm,
    lengths_ref,
    targets_ref,
    masks_ref,
    loss_ref,
    out_ref,
    returned,
    back_one_hot,
    sums_ref,
    send_one_hot,
    sent,
    relay,
    landed,
    meta_out,
    meta,
    codes,
    place_one_hot,
    return_one_hot,
    inverse,
    placed,
    queries,
    documents,
    partial,
    gathered,
    weights,
    gradients,
    returning,
    load_sem,
    send_sem,
    land_sem,
    meta_send_sem,
    meta_sem,
    spread_send_sem,
    spread_sem,
    side_send_sem,
    side_sem,
    score_send_sem,
    score_sem,
    weight_send_sem,
    weight_sem,
    far_send_sem,
    far_sem,
    back_send_sem,
    back_sem,
    relay_send_sem,
    relay_sem,
):
    blk = lax.axis_index("blk")
    dp = lax.axis_index("dp")
    home = lax.rem(blk, 8)
    part = mirror(home, blk // 8)
    ring = lax.rem(dp, 2) * 8 + (blk // 8) * 2 + dp // 2
    x, y = lax.rem(blk, 16) // 4, lax.rem(blk, 4)
    z, core = (dp // 2) * 2 + blk // 16, lax.rem(dp, 2)
    own_sum = lax.rem(x + y + z, 4)
    me = (own_sum * 2 + core) * 16 + x * 4 + y
    xs = [lax.rem(x + i, 4) for i in range(4)]
    ys = [lax.rem(y + j, 4) for j in range(4)]

    def class_peers(turn, to_core):
        zs = [lax.rem(z + turn + 4 - m, 4) for m in range(4)]
        zs = [lax.rem(v, 2) * 4 + v // 2 + to_core * 8 for v in zs]
        for i in range(4):
            for j in range(4):
                yield (
                    lax.rem(xs[i] + xs[i] // 2, 2) * 4 + ys[j],
                    (xs[i] // 2) * 2 + zs[(i + j) % 4],
                    xs[i] * 4 + ys[j],
                )

    def remote(src, dst, send, recv, to_part, to_ring):
        return pltpu.make_async_remote_copy(
            src_ref=src,
            dst_ref=dst,
            send_sem=send,
            recv_sem=recv,
            device_id=place(to_part, to_ring),
            device_id_type=MESH,
        )

    barrier = pltpu.get_barrier_semaphore()

    load = pltpu.make_async_copy(sums_hbm, sums_ref, load_sem)
    load.start()

    def greet(k, g):
        pl.semaphore_signal(barrier, inc=1, device_id=place(k, g), device_id_type=MESH)

    def greet_part(step, carry):
        k = lax.rem(part + step, GROUP)
        for g in range(RINGS):
            greet(k, g)
        return carry

    for turn in range(1, RINGS):
        greet(part, lax.rem(ring + turn, RINGS))
    lax.fori_loop(1, GROUP, greet_part, 0)

    target = targets_ref[...]
    length = lengths_ref[...].astype(F32)
    shard = target // ROWS
    slot = target % ROWS
    block = shard // 4
    to_ring = (shard % 2) * 8 + (block // 8) * 2 + (shard % 4) // 2
    of_shard = one_hot(iota((DEVICES, ROWS), 0) == shard)
    earlier = one_hot(iota((ROWS, ROWS), 0) < iota((ROWS, ROWS), 1))
    before = nn_dot(of_shard, earlier)
    rank = jnp.sum(before * of_shard.astype(F32), axis=0, keepdims=True).astype(jnp.int32)
    inner = (block % 8) * 2 + rank
    position = to_ring * MSG + inner
    send_one_hot[...] = one_hot(iota((2 * ROWS, ROWS), 0) == position)
    column = jnp.transpose(jnp.broadcast_to(position.astype(F32), (ROWS, ROWS))).astype(jnp.int32)
    lanes = iota((ROWS, ROWS), 1)
    back_one_hot[:, :ROWS] = one_hot(column == lanes)
    back_one_hot[:, ROWS:] = one_hot(column == lanes + ROWS)
    code = ((slot % 2) * PAIRS + slot // 2 + 1).astype(F32)
    mine = iota((RINGS, ROWS), 0) == to_ring
    spot = one_hot(iota((ROWS, ROWS), 0) == home * MSG + inner)
    code_rows = nt_dot(jnp.where(mine, code, 0.0).astype(BF16), spot)
    length_rows = nt_dot(jnp.where(mine, length, 0.0).astype(BF16), spot)
    for g in range(RINGS):
        meta_out[g, 0:1, :] = code_rows[g : g + 1]
        meta_out[g, 1:2, :] = length_rows[g : g + 1]
    scale = 1.0 / jnp.transpose(jnp.broadcast_to(length, (ROWS, ROWS)))
    scale = jnp.concatenate([scale] * (WIDE // ROWS), axis=1)

    def pack(k):
        columns = sums_ref[:, k * WIDE : (k + 1) * WIDE].astype(F32)
        embedded = (columns * scale).astype(BF16)
        sums_ref[:, k * WIDE : (k + 1) * WIDE] = embedded
        sent[k, :ROWS] = nn_dot(send_one_hot[:ROWS], embedded).astype(BF16)

    load.wait()
    for k in range(GROUP):
        pack(k)

    pl.semaphore_wait(barrier, DEVICES - 1)

    meta_dst = meta.at[part, me // 8]
    pltpu.make_async_copy(meta_out.at[ring], meta_dst, meta_sem).start()
    for turn in range(1, RINGS):
        g = lax.rem(ring + turn, RINGS)
        remote(meta_out.at[g], meta_dst, meta_send_sem, meta_sem, part, g).start()

    land_dst = landed.at[pl.ds(pl.multiple_of(me * MSG, MSG), MSG)]

    mate_dst = landed.at[pl.ds(pl.multiple_of((me - core * 16) * MSG, MSG), MSG)]
    hand_over = pltpu.make_async_remote_copy(
        src_ref=sent.at[:, pl.ds(ROWS, ROWS)],
        dst_ref=relay,
        send_sem=relay_send_sem.at[0],
        recv_sem=relay_sem,
        device_id=(blk, (dp // 2) * 2 + 1 - core),
        device_id_type=MESH,
    )

    def send_class(turn, to_core, source, dst, sem, stays):
        for index, (k, g, _) in enumerate(class_peers(turn, to_core)):
            src = source(k, g)
            if index == 0:

                @pl.when(stays)
                def _():
                    pltpu.make_async_copy(src, dst, land_sem.at[own_sum]).start()

                @pl.when(jnp.logical_not(stays))
                def _():
                    remote(src, dst, sem, land_sem.at[own_sum], k, g).start()

            else:
                remote(src, dst, sem, land_sem.at[own_sum], k, g).start()

    def sent_rows(k, g):
        return sent.at[k, pl.ds(pl.multiple_of(g * MSG, MSG), MSG)]

    def relay_rows(k, g):
        return relay.at[k, pl.ds(pl.multiple_of((g - GROUP) * MSG, MSG), MSG)]

    def rows_out(turn, carry):
        send_class(turn, 0, sent_rows, land_dst, send_sem, (turn == 0) & (core == 0))
        return carry

    def rows_on(turn, carry):
        send_class(turn, 1, sent_rows, land_dst, send_sem, turn == 0)
        send_class(turn, 1, relay_rows, mate_dst, relay_send_sem.at[1], turn == 0)
        return carry

    lax.fori_loop(0, 2, rows_out, 0)

    for k in range(GROUP):
        embedded = sums_ref[:, k * WIDE : (k + 1) * WIDE]
        sent[k, ROWS:] = nn_dot(send_one_hot[ROWS:], embedded).astype(BF16)

    @pl.when(core == 0)
    def _():
        hand_over.start()

    pltpu.make_async_copy(meta.at[part], meta.at[part], meta_sem).wait()

    others = [lax.rem(part + step, GROUP) for step in range(1, GROUP)]
    for k in others:
        remote(meta.at[part], meta.at[part], spread_send_sem, spread_sem, k, ring).start()

    lax.fori_loop(2, 4, rows_out, 0)

    @pl.when(core == 1)
    def _():
        hand_over.wait_recv()
        lax.fori_loop(0, 4, rows_on, 0)

    seven_meta = meta.at[pl.ds(0, GROUP - 1)]
    pltpu.make_async_copy(seven_meta, seven_meta, spread_sem).wait()
    both = meta[0]
    for k in range(1, GROUP):
        both = both + meta[k]
    codes[...] = both

    inner_shard = (iota((1, ROWS), 1) % MSG) // 2

    def full_slots(pair):
        raw = pair[0:1].astype(jnp.int32) - 1
        live = jnp.where(raw >= PAIRS, 7 * PAIRS + raw, raw) + inner_shard * PAIRS
        return jnp.where(raw >= 0, live, -1)

    def build(owners, carry):
        for q in range(4):
            full = full_slots(codes[4 * owners + q])
            place_one_hot[owners, :, q * ROWS : (q + 1) * ROWS] = one_hot(
                iota((8 * ROWS, ROWS), 0) == full
            )
        return carry

    lax.fori_loop(0, 4, build, 0)

    def build_return(a, carry):
        full = full_slots(codes[a]).astype(F32)
        down = jnp.transpose(jnp.broadcast_to(full, (ROWS, ROWS))).astype(jnp.int32)
        rows = pl.ds(pl.multiple_of(a * ROWS, ROWS), ROWS)
        for s in range(GROUP):
            return_one_hot[rows, s * ROWS : (s + 1) * ROWS] = one_hot(down == lanes + s * ROWS)
        return carry

    def build_inverse(block, carry):
        rows = pl.ds(pl.multiple_of(block * 256, 256), 256)
        total = None
        for owners in range(4):
            wide = jnp.concatenate([codes[4 * owners + q][1:2] for q in range(4)], axis=1)
            wide = jnp.broadcast_to(wide, (ROWS, 4 * ROWS)).astype(BF16)
            term = nt_dot(place_one_hot[owners, rows], wide)
            total = term if total is None else total + term
        inverse[rows] = coefficient / total
        return carry

    lax.fori_loop(0, 16, build_return, 0)
    lax.fori_loop(0, 4, build_inverse, 0)

    after = core * 8 + lax.rem(lax.rem(ring, 8) + 2, 8)
    ahead = core * 8 + lax.rem(lax.rem(ring, 8) + 6, 8)
    to_next = remote(
        documents.at[8 * PAIRS :], documents.at[:PAIRS], side_send_sem.at[0], side_sem.at[0], part, after
    )
    to_last = remote(
        queries.at[:PAIRS], queries.at[8 * PAIRS :], side_send_sem.at[1], side_sem.at[1], part, ahead
    )

    def land(step):
        owners = lax.rem(own_sum + 4 - step, 4)
        rows = pl.ds(pl.multiple_of(owners * 512, 512), 512)
        pltpu.make_async_copy(landed.at[rows], landed.at[rows], land_sem.at[owners]).wait()
        return owners, rows

    def put(now, block):
        owners, rows = now
        return nn_dot(place_one_hot[owners, block * 256 : (block + 1) * 256], landed[rows])

    first = land(0)
    for block in range(4):
        placed[block * 256 : (block + 1) * 256] = put(first, block)

    def put_more(step, carry):
        now = land(step)
        for block in range(4):
            slots = pl.ds(block * 256, 256)
            placed[slots] = placed[slots] + put(now, block)
        return carry

    lax.fori_loop(1, 3, put_more, 0)
    last = land(3)
    documents[320:576] = (placed[768:1024] + put(last, 3)).astype(BF16)
    to_next.start()
    queries[0:256] = (placed[0:256] + put(last, 0)).astype(BF16)
    to_last.start()
    queries[256:512] = (placed[256:512] + put(last, 1)).astype(BF16)
    documents[64:320] = (placed[512:768] + put(last, 2)).astype(BF16)

    def score(s):
        return nt_dot(
            queries[s * PAIRS : (s + 1) * PAIRS], documents[s * PAIRS : (s + 2) * PAIRS]
        )

    def score_out(s):
        return remote(
            partial.at[s],
            gathered.at[part],
            score_send_sem,
            score_sem,
            mirror(s, blk // 8),
            ring,
        )

    for s in range(1, GROUP):
        partial[s] = score(s)
    for k in others:
        s = mirror(k, blk // 8)

        @pl.when(s != 0)
        def _():
            score_out(s).start()

    to_next.wait_recv()
    partial[0] = score(0)

    @pl.when(home != 0)
    def _():
        score_out(0).start()

    gathered[part] = partial[home]

    row = iota((PAIRS, 2 * PAIRS), 0)
    col = iota((PAIRS, 2 * PAIRS), 1)

    def tile(stop, i, j):
        return masks_ref[0, stop, i, j]

    top = jnp.where(
        col < 32,
        tile(1, 0, 0),
        jnp.where(col < 64, tile(1, 0, 1), jnp.where(col < 96, 1, tile(0, 0, 1))),
    )
    low = jnp.where(
        col < 32,
        tile(1, 1, 0),
        jnp.where(col < 64, tile(1, 1, 1), jnp.where(col < 96, tile(0, 1, 0), 1)),
    )
    live = jnp.where(row < 32, top, low) > 0
    seven_scores = gathered.at[pl.ds(0, GROUP - 1)]
    pltpu.make_async_copy(seven_scores, seven_scores, score_sem).wait()
    scores = gathered[0]
    for k in range(1, GROUP):
        scores = scores + gathered[k]
    scores = factor * scores

    masked = jnp.where(live, scores, -jnp.inf)
    highest = jnp.max(masked, axis=1, keepdims=True)
    shares = jnp.exp(masked - highest)
    share_total = jnp.sum(shares, axis=1, keepdims=True)
    weights[home] = (shares * (1.0 / share_total)).astype(BF16)

    @pl.when(home == 0)
    def _():
        for k in range(GROUP):
            remote(weights.at[0], weights.at[8], far_send_sem, far_sem, k, ahead).start()

    for k in others:
        remote(weights.at[home], weights.at[home], weight_send_sem, weight_sem, k, ring).start()

    log_total = highest + jnp.log(share_total)
    diagonal = jnp.sum(jnp.where(col == row + PAIRS, scores, 0.0), axis=1, keepdims=True)
    losses = jnp.where(col == row, log_total - diagonal, 0.0)
    loss_ref[...] = jnp.sum(losses, axis=0, keepdims=True)[:, :PAIRS]
    seven_weights = weights.at[pl.ds(0, GROUP - 1)]
    pltpu.make_async_copy(seven_weights, seven_weights, weight_sem).wait()

    def spread_scale(value):
        return jnp.concatenate([value] * (WIDE // ROWS), axis=1)

    def rows_of(s):
        return slice(s * PAIRS, (s + 1) * PAIRS)

    held = None
    for s in range(GROUP + 1):
        if s == GROUP:
            to_last.wait_recv()
            pltpu.make_async_copy(weights.at[s], weights.at[s], far_sem).wait()
        weight = weights[s]
        far = tn_dot(weight, queries[rows_of(s)])
        if s > 0:
            slots = rows_of(GROUP + s - 1)
            gradients[slots] = ((held + far[:PAIRS]) * spread_scale(inverse[slots])).astype(BF16)
        if s < GROUP:
            held = far[PAIRS:] - queries[rows_of(s)].astype(F32)
            own = rows_of(s)
            term = nn_dot(weight, documents[s * PAIRS : (s + 2) * PAIRS])
            term = term - documents[rows_of(s + 1)].astype(F32)
            gradients[own] = (term * spread_scale(inverse[own])).astype(BF16)

    back_dst = returned.at[part, pl.ds(pl.multiple_of(ring * MSG, MSG), MSG)]

    def back_rows(label, spot):
        return returning.at[pl.ds(pl.multiple_of((label * 16 + spot) * MSG, MSG), MSG)]

    def rows_back(step, carry):
        turn, to_core = lax.rem(step, 4), lax.rem(step // 4 + core, 2)
        label = lax.rem(own_sum + turn, 4) * 2 + to_core
        rows = pl.ds(pl.multiple_of(label * 256, 256), 256)
        returning[rows] = nn_dot(return_one_hot[rows], gradients[...]).astype(BF16)
        for index, (k, g, spot) in enumerate(class_peers(turn, to_core)):
            src = back_rows(label, spot)
            if index == 0:
                stays = (turn == 0) & (to_core == core)

                @pl.when(stays)
                def _():
                    pltpu.make_async_copy(src, back_dst, back_sem.at[part]).start()

                @pl.when(jnp.logical_not(stays))
                def _():
                    remote(src, back_dst, back_send_sem, back_sem.at[part], k, g).start()

            else:
                remote(src, back_dst, back_send_sem, back_sem.at[part], k, g).start()
        return carry

    lax.fori_loop(0, 8, rows_back, 0)

    def finish(step, carry):
        k = lax.rem(part + GROUP - step, GROUP)
        pltpu.make_async_copy(returned.at[k], returned.at[k], back_sem.at[k]).wait()
        out_ref[:, pl.ds(pl.multiple_of(k * WIDE, WIDE), WIDE)] = nn_dot(
            back_one_hot[...], returned[k]
        ).astype(BF16)
        return carry

    lax.fori_loop(0, GROUP, finish, 0)

    most = landed.at[pl.ds(0, (DEVICES - 1) * MSG)]
    half = landed.at[pl.ds(0, (PAIRS - 1) * MSG)]

    @pl.when(core == 0)
    def _():
        hand_over.wait_send()
        pltpu.make_async_copy(half, half, send_sem).wait()

    @pl.when(core == 1)
    def _():
        pltpu.make_async_copy(most, most, send_sem).wait()
        pltpu.make_async_copy(half, half, relay_send_sem.at[1]).wait()

    pltpu.make_async_copy(most, most, back_send_sem).wait()
    fifteen = meta_out.at[pl.ds(0, RINGS - 1)]
    pltpu.make_async_copy(fifteen, fifteen, meta_send_sem).wait()
    to_next.wait_send()
    to_last.wait_send()

    pltpu.make_async_copy(seven_meta, seven_meta, spread_send_sem).wait()
    pltpu.make_async_copy(seven_scores, seven_scores, score_send_sem).wait()
    pltpu.make_async_copy(seven_weights, seven_weights, weight_send_sem).wait()

    @pl.when(home == 0)
    def _():
        eight_weights = weights.at[pl.ds(0, GROUP)]
        pltpu.make_async_copy(eight_weights, eight_weights, far_send_sem).wait()


def finish_kernel(loss_in, rows_in, loss_ref, out_ref):
    loss_ref[...] = loss_in[...]
    out_ref[...] = rows_in[...]


def local(segment_sums, lengths, targets, tile_masks):
    width = segment_sums.shape[1]
    factor = 16.0 / math.sqrt(width)
    coefficient = factor / (PAIRS * DEVICES)
    vmem = pl.BlockSpec(memory_space=pltpu.VMEM)
    smem = pl.BlockSpec(memory_space=pltpu.SMEM)
    dma = pltpu.SemaphoreType.DMA
    results = pl.pallas_call(
        functools.partial(kernel, factor, coefficient),
        out_shape=(
            jax.ShapeDtypeStruct((1, PAIRS), F32),
            jax.ShapeDtypeStruct((ROWS, width), BF16),
        ),
        in_specs=[pl.BlockSpec(memory_space=pl.ANY), vmem, vmem, smem],
        out_specs=(vmem, vmem),
        scratch_shapes=[
            pltpu.VMEM((GROUP, 2 * ROWS, WIDE), BF16),
            pltpu.VMEM((ROWS, 2 * ROWS), BF16),
            pltpu.VMEM((ROWS, width), BF16),
            pltpu.VMEM((2 * ROWS, ROWS), BF16),
            pltpu.VMEM((GROUP, 2 * ROWS, WIDE), BF16),
            pltpu.VMEM((GROUP, ROWS, WIDE), BF16),
            pltpu.VMEM((DEVICES * MSG, WIDE), BF16),
            pltpu.VMEM((RINGS, 2, ROWS), F32),
            pltpu.VMEM((GROUP, 16, 2, ROWS), F32),
            pltpu.VMEM((16, 2, ROWS), F32),
            pltpu.VMEM((4, GROUP * ROWS, 4 * ROWS), BF16),
            pltpu.VMEM((DEVICES * MSG, GROUP * ROWS), BF16),
            pltpu.VMEM((GROUP * ROWS, ROWS), F32),
            pltpu.VMEM((16 * PAIRS, WIDE), F32),
            pltpu.VMEM((9 * PAIRS, WIDE), BF16),
            pltpu.VMEM((9 * PAIRS, WIDE), BF16),
            pltpu.VMEM((GROUP, PAIRS, 2 * PAIRS), F32),
            pltpu.VMEM((GROUP, PAIRS, 2 * PAIRS), F32),
            pltpu.VMEM((9, PAIRS, 2 * PAIRS), BF16),
            pltpu.VMEM((16 * PAIRS, WIDE), BF16),
            pltpu.VMEM((DEVICES * MSG, WIDE), BF16),
            dma,
            dma,
            dma((4,)),
            dma,
            dma,
            dma,
            dma,
            dma((2,)),
            dma((2,)),
            dma,
            dma,
            dma,
            dma,
            dma,
            dma,
            dma,
            dma((GROUP,)),
            dma((2,)),
            dma,
        ],
        compiler_params=pltpu.CompilerParams(
            collective_id=0, has_side_effects=True, vmem_limit_bytes=56 << 20
        ),
    )(segment_sums, lengths.reshape(1, ROWS), targets.reshape(1, ROWS), tile_masks)
    losses, gradients = pl.pallas_call(
        finish_kernel,
        out_shape=(
            jax.ShapeDtypeStruct((1, PAIRS), F32),
            jax.ShapeDtypeStruct((ROWS, width), BF16),
        ),
        in_specs=[vmem, vmem],
        out_specs=(vmem, vmem),
    )(*results)
    return losses.reshape(PAIRS), gradients


def solution(mesh):
    in_specs = (
        P(("blk", "dp"), None),
        P(("blk", "dp")),
        P(("blk", "dp")),
        P(("blk", "dp"), None, None, None),
    )
    out_specs = (P(("blk", "dp")), P(("blk", "dp"), None))
    return jax.shard_map(local, mesh=mesh, in_specs=in_specs, out_specs=out_specs, check_vma=False)
```

```python
import functools
import math

import jax
import jax.numpy as jnp
from jax import lax
from jax.experimental import pallas as pl
from jax.experimental.pallas import tpu as pltpu
from jax.sharding import PartitionSpec as P

MESH = pl.DeviceIdType.MESH
GROUP = 8
WIDE = 512
RINGS = 16
DEVICES = 128
ROWS = 128
PAIRS = 64
MSG = 16
F32 = jnp.float32
BF16 = jnp.bfloat16


def iota(shape, dim):
    return lax.broadcasted_iota(jnp.int32, shape, dim)


def nt_dot(a, b):
    return lax.dot_general(a, b, (((1,), (1,)), ((), ())), preferred_element_type=F32)


def tn_dot(a, b):
    return lax.dot_general(a, b, (((0,), (0,)), ((), ())), preferred_element_type=F32)


def nn_dot(a, b):
    return jnp.dot(a, b, preferred_element_type=F32)


def one_hot(mask):
    return jnp.where(mask, 1.0, 0.0).astype(BF16)


def mirror(part, group):
    return lax.rem(part // 4 + group, 2) * 4 + lax.rem(part, 4)


def place(part, ring):
    group = lax.rem(ring, 8) // 2
    return group * 8 + mirror(part, group), lax.rem(ring, 2) * 2 + ring // 8


def kernel(
    factor,
    coefficient,
    sums_hbm,
    lengths_ref,
    targets_ref,
    masks_ref,
    loss_ref,
    returned,
    back_one_hot,
    sums_ref,
    send_one_hot,
    sent,
    relay,
    landed,
    meta_out,
    meta,
    codes,
    place_one_hot,
    return_one_hot,
    inverse,
    placed,
    queries,
    documents,
    partial,
    gathered,
    weights,
    gradients,
    returning,
    load_sem,
    send_sem,
    land_sem,
    meta_send_sem,
    meta_sem,
    spread_send_sem,
    spread_sem,
    side_send_sem,
    side_sem,
    score_send_sem,
    score_sem,
    weight_send_sem,
    weight_sem,
    far_send_sem,
    far_sem,
    back_send_sem,
    back_sem,
    relay_send_sem,
    relay_sem,
):
    blk = lax.axis_index("blk")
    dp = lax.axis_index("dp")
    home = lax.rem(blk, 8)
    part = mirror(home, blk // 8)
    ring = lax.rem(dp, 2) * 8 + (blk // 8) * 2 + dp // 2
    x, y = lax.rem(blk, 16) // 4, lax.rem(blk, 4)
    z, core = (dp // 2) * 2 + blk // 16, lax.rem(dp, 2)
    own_sum = lax.rem(x + y + z, 4)
    me = (own_sum * 2 + core) * 16 + x * 4 + y
    xs = [lax.rem(x + i, 4) for i in range(4)]
    ys = [lax.rem(y + j, 4) for j in range(4)]

    def class_peers(turn, to_core):
        zs = [lax.rem(z + turn + 4 - m, 4) for m in range(4)]
        zs = [lax.rem(v, 2) * 4 + v // 2 + to_core * 8 for v in zs]
        for i in range(4):
            for j in range(4):
                yield (
                    lax.rem(xs[i] + xs[i] // 2, 2) * 4 + ys[j],
                    (xs[i] // 2) * 2 + zs[(i + j) % 4],
                    xs[i] * 4 + ys[j],
                )

    def remote(src, dst, send, recv, to_part, to_ring):
        return pltpu.make_async_remote_copy(
            src_ref=src,
            dst_ref=dst,
            send_sem=send,
            recv_sem=recv,
            device_id=place(to_part, to_ring),
            device_id_type=MESH,
        )

    barrier = pltpu.get_barrier_semaphore()

    load = pltpu.make_async_copy(sums_hbm, sums_ref, load_sem)
    load.start()

    def greet(k, g):
        pl.semaphore_signal(barrier, inc=1, device_id=place(k, g), device_id_type=MESH)

    def greet_part(step, carry):
        k = lax.rem(part + step, GROUP)
        for g in range(RINGS):
            greet(k, g)
        return carry

    for turn in range(1, RINGS):
        greet(part, lax.rem(ring + turn, RINGS))
    for step in range(1, GROUP):
        greet_part(step, 0)

    target = targets_ref[...]
    length = lengths_ref[...].astype(F32)
    shard = target // ROWS
    slot = target % ROWS
    block = shard // 4
    to_ring = (shard % 2) * 8 + (block // 8) * 2 + (shard % 4) // 2
    of_shard = one_hot(iota((DEVICES, ROWS), 0) == shard)
    earlier = one_hot(iota((ROWS, ROWS), 0) < iota((ROWS, ROWS), 1))
    before = nn_dot(of_shard, earlier)
    rank = jnp.sum(before * of_shard.astype(F32), axis=0, keepdims=True).astype(jnp.int32)
    inner = (block % 8) * 2 + rank
    position = to_ring * MSG + inner
    send_one_hot[...] = one_hot(iota((2 * ROWS, ROWS), 0) == position)
    column = jnp.transpose(jnp.broadcast_to(position.astype(F32), (ROWS, ROWS))).astype(jnp.int32)
    lanes = iota((ROWS, ROWS), 1)
    back_one_hot[:, :ROWS] = one_hot(column == lanes)
    back_one_hot[:, ROWS:] = one_hot(column == lanes + ROWS)
    code = ((slot % 2) * PAIRS + slot // 2 + 1).astype(F32)
    mine = iota((RINGS, ROWS), 0) == to_ring
    spot = one_hot(iota((ROWS, ROWS), 0) == home * MSG + inner)
    code_rows = nt_dot(jnp.where(mine, code, 0.0).astype(BF16), spot)
    length_rows = nt_dot(jnp.where(mine, length, 0.0).astype(BF16), spot)
    for g in range(RINGS):
        meta_out[g, 0:1, :] = code_rows[g : g + 1]
        meta_out[g, 1:2, :] = length_rows[g : g + 1]
    scale = 1.0 / jnp.transpose(jnp.broadcast_to(length, (ROWS, ROWS)))
    scale = jnp.concatenate([scale] * (WIDE // ROWS), axis=1)

    def pack(k):
        columns = sums_ref[:, k * WIDE : (k + 1) * WIDE].astype(F32)
        embedded = (columns * scale).astype(BF16)
        sent[k] = nn_dot(send_one_hot[...], embedded).astype(BF16)

    load.wait()
    for k in range(GROUP):
        pack(k)

    pl.semaphore_wait(barrier, DEVICES - 1)

    meta_dst = meta.at[part, me // 8]
    pltpu.make_async_copy(meta_out.at[ring], meta_dst, meta_sem).start()
    for turn in range(1, RINGS):
        g = lax.rem(ring + turn, RINGS)
        remote(meta_out.at[g], meta_dst, meta_send_sem, meta_sem, part, g).start()

    land_dst = landed.at[pl.ds(pl.multiple_of(me * MSG, MSG), MSG)]

    mate_dst = landed.at[pl.ds(pl.multiple_of((me - core * 16) * MSG, MSG), MSG)]
    hand_over = pltpu.make_async_remote_copy(
        src_ref=sent.at[:, pl.ds(ROWS, ROWS)],
        dst_ref=relay,
        send_sem=relay_send_sem.at[0],
        recv_sem=relay_sem,
        device_id=(blk, (dp // 2) * 2 + 1 - core),
        device_id_type=MESH,
    )

    def send_class(turn, to_core, source, dst, sem, stays):
        for index, (k, g, _) in enumerate(class_peers(turn, to_core)):
            src = source(k, g)
            if index == 0:

                @pl.when(stays)
                def _():
                    pltpu.make_async_copy(src, dst, land_sem.at[own_sum]).start()

                @pl.when(jnp.logical_not(stays))
                def _():
                    remote(src, dst, sem, land_sem.at[own_sum], k, g).start()

            else:
                remote(src, dst, sem, land_sem.at[own_sum], k, g).start()

    def sent_rows(k, g):
        return sent.at[k, pl.ds(pl.multiple_of(g * MSG, MSG), MSG)]

    def relay_rows(k, g):
        return relay.at[k, pl.ds(pl.multiple_of((g - GROUP) * MSG, MSG), MSG)]

    def rows_out(turn, carry):
        send_class(turn, 0, sent_rows, land_dst, send_sem, (turn == 0) & (core == 0))
        return carry

    def rows_on(turn, carry):
        send_class(turn, 1, sent_rows, land_dst, send_sem, turn == 0)
        send_class(turn, 1, relay_rows, mate_dst, relay_send_sem.at[1], turn == 0)
        return carry

    lax.fori_loop(0, 2, rows_out, 0)

    @pl.when(core == 0)
    def _():
        hand_over.start()

    pltpu.make_async_copy(meta.at[part], meta.at[part], meta_sem).wait()

    others = [lax.rem(part + step, GROUP) for step in range(1, GROUP)]
    for k in others:
        remote(meta.at[part], meta.at[part], spread_send_sem, spread_sem, k, ring).start()

    lax.fori_loop(2, 4, rows_out, 0)

    @pl.when(core == 1)
    def _():
        hand_over.wait_recv()
        lax.fori_loop(0, 4, rows_on, 0)

    seven_meta = meta.at[pl.ds(0, GROUP - 1)]
    pltpu.make_async_copy(seven_meta, seven_meta, spread_sem).wait()
    both = meta[0]
    for k in range(1, GROUP):
        both = both + meta[k]
    codes[...] = both

    inner_shard = (iota((1, ROWS), 1) % MSG) // 2

    def full_slots(pair):
        raw = pair[0:1].astype(jnp.int32) - 1
        live = jnp.where(raw >= PAIRS, 7 * PAIRS + raw, raw) + inner_shard * PAIRS
        return jnp.where(raw >= 0, live, -1)

    def build(owners, carry):
        for q in range(4):
            full = full_slots(codes[4 * owners + q])
            place_one_hot[owners, :, q * ROWS : (q + 1) * ROWS] = one_hot(
                iota((8 * ROWS, ROWS), 0) == full
            )
        return carry

    lax.fori_loop(0, 4, build, 0)

    def build_return(a, carry):
        full = full_slots(codes[a]).astype(F32)
        down = jnp.transpose(jnp.broadcast_to(full, (ROWS, ROWS))).astype(jnp.int32)
        rows = pl.ds(pl.multiple_of(a * ROWS, ROWS), ROWS)
        for s in range(GROUP):
            return_one_hot[rows, s * ROWS : (s + 1) * ROWS] = one_hot(down == lanes + s * ROWS)
        return carry

    def build_inverse(block, carry):
        rows = pl.ds(pl.multiple_of(block * 256, 256), 256)
        total = None
        for owners in range(4):
            wide = jnp.concatenate([codes[4 * owners + q][1:2] for q in range(4)], axis=1)
            wide = jnp.broadcast_to(wide, (ROWS, 4 * ROWS)).astype(BF16)
            term = nt_dot(place_one_hot[owners, rows], wide)
            total = term if total is None else total + term
        inverse[rows] = coefficient / total
        return carry

    lax.fori_loop(0, 16, build_return, 0)
    lax.fori_loop(0, 4, build_inverse, 0)

    after = core * 8 + lax.rem(lax.rem(ring, 8) + 2, 8)
    ahead = core * 8 + lax.rem(lax.rem(ring, 8) + 6, 8)
    to_next = remote(
        documents.at[8 * PAIRS :], documents.at[:PAIRS], side_send_sem.at[0], side_sem.at[0], part, after
    )
    to_last = remote(
        queries.at[:PAIRS], queries.at[8 * PAIRS :], side_send_sem.at[1], side_sem.at[1], part, ahead
    )

    def land(step):
        owners = lax.rem(own_sum + 4 - step, 4)
        rows = pl.ds(pl.multiple_of(owners * 512, 512), 512)
        pltpu.make_async_copy(landed.at[rows], landed.at[rows], land_sem.at[owners]).wait()
        return owners, rows

    def put(now, block):
        owners, rows = now
        return nn_dot(place_one_hot[owners, block * 256 : (block + 1) * 256], landed[rows])

    first = land(0)
    for block in range(4):
        placed[block * 256 : (block + 1) * 256] = put(first, block)

    def put_more(step, carry):
        now = land(step)
        for block in range(4):
            slots = pl.ds(block * 256, 256)
            placed[slots] = placed[slots] + put(now, block)
        return carry

    lax.fori_loop(1, 3, put_more, 0)
    last = land(3)
    documents[320:576] = (placed[768:1024] + put(last, 3)).astype(BF16)
    to_next.start()
    queries[0:256] = (placed[0:256] + put(last, 0)).astype(BF16)
    to_last.start()
    queries[256:512] = (placed[256:512] + put(last, 1)).astype(BF16)
    documents[64:320] = (placed[512:768] + put(last, 2)).astype(BF16)

    def score(s):
        return nt_dot(
            queries[s * PAIRS : (s + 1) * PAIRS], documents[s * PAIRS : (s + 2) * PAIRS]
        )

    def score_out(s):
        return remote(
            partial.at[s],
            gathered.at[part],
            score_send_sem,
            score_sem,
            mirror(s, blk // 8),
            ring,
        )

    for s in range(1, GROUP):
        partial[s] = score(s)
    for k in others:
        s = mirror(k, blk // 8)

        @pl.when(s != 0)
        def _():
            score_out(s).start()

    to_next.wait_recv()
    partial[0] = score(0)

    @pl.when(home != 0)
    def _():
        score_out(0).start()

    gathered[part] = partial[home]

    row = iota((PAIRS, 2 * PAIRS), 0)
    col = iota((PAIRS, 2 * PAIRS), 1)

    def tile(stop, i, j):
        return masks_ref[0, stop, i, j]

    top = jnp.where(
        col < 32,
        tile(1, 0, 0),
        jnp.where(col < 64, tile(1, 0, 1), jnp.where(col < 96, 1, tile(0, 0, 1))),
    )
    low = jnp.where(
        col < 32,
        tile(1, 1, 0),
        jnp.where(col < 64, tile(1, 1, 1), jnp.where(col < 96, tile(0, 1, 0), 1)),
    )
    live = jnp.where(row < 32, top, low) > 0
    seven_scores = gathered.at[pl.ds(0, GROUP - 1)]
    pltpu.make_async_copy(seven_scores, seven_scores, score_sem).wait()
    scores = gathered[0]
    for k in range(1, GROUP):
        scores = scores + gathered[k]
    scores = factor * scores

    masked = jnp.where(live, scores, -jnp.inf)
    highest = jnp.max(masked, axis=1, keepdims=True)
    shares = jnp.exp(masked - highest)
    share_total = jnp.sum(shares, axis=1, keepdims=True)
    weights[home] = (shares * (1.0 / share_total)).astype(BF16)

    @pl.when(home == 0)
    def _():
        for k in range(GROUP):
            remote(weights.at[0], weights.at[8], far_send_sem, far_sem, k, ahead).start()

    for k in others:
        remote(weights.at[home], weights.at[home], weight_send_sem, weight_sem, k, ring).start()

    log_total = highest + jnp.log(share_total)
    diagonal = jnp.sum(jnp.where(col == row + PAIRS, scores, 0.0), axis=1, keepdims=True)
    losses = jnp.where(col == row, log_total - diagonal, 0.0)
    loss_ref[...] = jnp.sum(losses, axis=0, keepdims=True)[:, :PAIRS]
    seven_weights = weights.at[pl.ds(0, GROUP - 1)]
    pltpu.make_async_copy(seven_weights, seven_weights, weight_sem).wait()

    def spread_scale(value):
        return jnp.concatenate([value] * (WIDE // ROWS), axis=1)

    def rows_of(s):
        return slice(s * PAIRS, (s + 1) * PAIRS)

    held = None
    for s in range(GROUP + 1):
        if s == GROUP:
            to_last.wait_recv()
            pltpu.make_async_copy(weights.at[s], weights.at[s], far_sem).wait()
        weight = weights[s]
        far = tn_dot(weight, queries[rows_of(s)])
        if s > 0:
            slots = rows_of(GROUP + s - 1)
            gradients[slots] = ((held + far[:PAIRS]) * spread_scale(inverse[slots])).astype(BF16)
        if s < GROUP:
            held = far[PAIRS:] - queries[rows_of(s)].astype(F32)
            own = rows_of(s)
            term = nn_dot(weight, documents[s * PAIRS : (s + 2) * PAIRS])
            term = term - documents[rows_of(s + 1)].astype(F32)
            gradients[own] = (term * spread_scale(inverse[own])).astype(BF16)

    back_dst = returned.at[part, pl.ds(pl.multiple_of(ring * MSG, MSG), MSG)]

    def back_rows(label, spot):
        return returning.at[pl.ds(pl.multiple_of((label * 16 + spot) * MSG, MSG), MSG)]

    def rows_back(step, carry):
        turn, to_core = lax.rem(step, 4), lax.rem(step // 4 + core, 2)
        label = lax.rem(own_sum + turn, 4) * 2 + to_core
        rows = pl.ds(pl.multiple_of(label * 256, 256), 256)
        returning[rows] = nn_dot(return_one_hot[rows], gradients[...]).astype(BF16)
        for index, (k, g, spot) in enumerate(class_peers(turn, to_core)):
            src = back_rows(label, spot)
            if index == 0:
                stays = (turn == 0) & (to_core == core)

                @pl.when(stays)
                def _():
                    pltpu.make_async_copy(src, back_dst, back_sem.at[part]).start()

                @pl.when(jnp.logical_not(stays))
                def _():
                    remote(src, back_dst, back_send_sem, back_sem.at[part], k, g).start()

            else:
                remote(src, back_dst, back_send_sem, back_sem.at[part], k, g).start()
        return carry

    lax.fori_loop(0, 8, rows_back, 0)

    def finish(step, carry):
        k = lax.rem(part + GROUP - step, GROUP)
        pltpu.make_async_copy(returned.at[k], returned.at[k], back_sem.at[k]).wait()
        return carry

    lax.fori_loop(0, GROUP, finish, 0)

    most = landed.at[pl.ds(0, (DEVICES - 1) * MSG)]
    half = landed.at[pl.ds(0, (PAIRS - 1) * MSG)]

    @pl.when(core == 0)
    def _():
        hand_over.wait_send()
        pltpu.make_async_copy(half, half, send_sem).wait()

    @pl.when(core == 1)
    def _():
        pltpu.make_async_copy(most, most, send_sem).wait()
        pltpu.make_async_copy(half, half, relay_send_sem.at[1]).wait()

    pltpu.make_async_copy(most, most, back_send_sem).wait()
    fifteen = meta_out.at[pl.ds(0, RINGS - 1)]
    pltpu.make_async_copy(fifteen, fifteen, meta_send_sem).wait()
    to_next.wait_send()
    to_last.wait_send()

    pltpu.make_async_copy(seven_meta, seven_meta, spread_send_sem).wait()
    pltpu.make_async_copy(seven_scores, seven_scores, score_send_sem).wait()
    pltpu.make_async_copy(seven_weights, seven_weights, weight_send_sem).wait()

    @pl.when(home == 0)
    def _():
        eight_weights = weights.at[pl.ds(0, GROUP)]
        pltpu.make_async_copy(eight_weights, eight_weights, far_send_sem).wait()


def finish_kernel(loss_in, returned, back_one_hot, loss_ref, out_ref):
    loss_ref[...] = loss_in[...]
    for k in range(GROUP):
        out_ref[:, k * WIDE : (k + 1) * WIDE] = nn_dot(back_one_hot[...], returned[k]).astype(BF16)


def local(segment_sums, lengths, targets, tile_masks):
    width = segment_sums.shape[1]
    factor = 16.0 / math.sqrt(width)
    coefficient = factor / (PAIRS * DEVICES)
    vmem = pl.BlockSpec(memory_space=pltpu.VMEM)
    smem = pl.BlockSpec(memory_space=pltpu.SMEM)
    dma = pltpu.SemaphoreType.DMA
    results = pl.pallas_call(
        functools.partial(kernel, factor, coefficient),
        out_shape=(
            jax.ShapeDtypeStruct((1, PAIRS), F32),
            jax.ShapeDtypeStruct((GROUP, 2 * ROWS, WIDE), BF16),
            jax.ShapeDtypeStruct((ROWS, 2 * ROWS), BF16),
        ),
        in_specs=[pl.BlockSpec(memory_space=pl.ANY), vmem, vmem, smem],
        out_specs=(vmem, vmem, vmem),
        scratch_shapes=[
            pltpu.VMEM((ROWS, width), BF16),
            pltpu.VMEM((2 * ROWS, ROWS), BF16),
            pltpu.VMEM((GROUP, 2 * ROWS, WIDE), BF16),
            pltpu.VMEM((GROUP, ROWS, WIDE), BF16),
            pltpu.VMEM((DEVICES * MSG, WIDE), BF16),
            pltpu.VMEM((RINGS, 2, ROWS), F32),
            pltpu.VMEM((GROUP, 16, 2, ROWS), F32),
            pltpu.VMEM((16, 2, ROWS), F32),
            pltpu.VMEM((4, GROUP * ROWS, 4 * ROWS), BF16),
            pltpu.VMEM((DEVICES * MSG, GROUP * ROWS), BF16),
            pltpu.VMEM((GROUP * ROWS, ROWS), F32),
            pltpu.VMEM((16 * PAIRS, WIDE), F32),
            pltpu.VMEM((9 * PAIRS, WIDE), BF16),
            pltpu.VMEM((9 * PAIRS, WIDE), BF16),
            pltpu.VMEM((GROUP, PAIRS, 2 * PAIRS), F32),
            pltpu.VMEM((GROUP, PAIRS, 2 * PAIRS), F32),
            pltpu.VMEM((9, PAIRS, 2 * PAIRS), BF16),
            pltpu.VMEM((16 * PAIRS, WIDE), BF16),
            pltpu.VMEM((DEVICES * MSG, WIDE), BF16),
            dma,
            dma,
            dma((4,)),
            dma,
            dma,
            dma,
            dma,
            dma((2,)),
            dma((2,)),
            dma,
            dma,
            dma,
            dma,
            dma,
            dma,
            dma,
            dma((GROUP,)),
            dma((2,)),
            dma,
        ],
        compiler_params=pltpu.CompilerParams(
            collective_id=0, has_side_effects=True, vmem_limit_bytes=56 << 20
        ),
    )(segment_sums, lengths.reshape(1, ROWS), targets.reshape(1, ROWS), tile_masks)
    losses, gradients = pl.pallas_call(
        finish_kernel,
        out_shape=(
            jax.ShapeDtypeStruct((1, PAIRS), F32),
            jax.ShapeDtypeStruct((ROWS, width), BF16),
        ),
        in_specs=[vmem, vmem, vmem],
        out_specs=(vmem, vmem),
    )(*results)
    return losses.reshape(PAIRS), gradients


def solution(mesh):
    in_specs = (
        P(("blk", "dp"), None),
        P(("blk", "dp")),
        P(("blk", "dp")),
        P(("blk", "dp"), None, None, None),
    )
    out_specs = (P(("blk", "dp")), P(("blk", "dp"), None))
    return jax.shard_map(local, mesh=mesh, in_specs=in_specs, out_specs=out_specs, check_vma=False)
```
